128 devices in a mesh: rows: 16 (over z, x_lo, core), cols: 8 (over y, x_hi).
Axes of the slice: x: 4 (x_hi: 2, x_lo: 2; x = x_hi * 2 + x_lo), y: 4, z: 4, core: 2. Of those that a mesh axis runs over, the one named last changes fastest.
Arguments:
- fine_input: bfloat16 [2048, 2048, 64], P('rows', 'cols'), may hold values from -6 to 6
- cotangent: bfloat16 [2048, 2048, 64], P('rows', 'cols'), may hold values from -6 to 6
- lift_weight: bfloat16 [64, 256], replicated, may hold values from -3 to 3
- spectral_weight: bfloat16 [2, 512, 256, 256], P(None, ('rows', 'cols')), may hold values from -6 to 6
- skip_weight: bfloat16 [256, 256], replicated, may hold values from -0.375 to 0.375
- down_weight: bfloat16 [256, 64], replicated, may hold values from -0.375 to 0.375
- skip_fine: bfloat16 [64, 64], replicated, may hold values from -0.75 to 0.75
Outputs:
- grad_input: bfloat16 [2048, 2048, 64], P('rows', 'cols')
- grad_spectral: float32 [2, 512, 256, 256], P(None, ('rows', 'cols'))
- grad_lift: float32 [64, 256], replicated
- grad_skip: float32 [256, 256], replicated
- grad_down: float32 [256, 64], replicated
- grad_fine_skip: float32 [64, 64], replicated
The draws below stay inside these ranges and needn't reach their ends.
All inputs are finite; a program needn't handle non-finite values.
Results may differ from the reference program's by a relative error of at most 0.018.
Values sent between devices are 32-bit elements; how exact they have to be, the bound alone decides.
No kernel may reach another device: no remote copies, remote signals or barrier semaphores. Data moves between devices by JAX's collectives and lax.ppermute only.
A program may use at most 128 MiB of HBM per device.

```python
import math
import jax
import jax.numpy as jnp
from jax import lax

C = 64
CC = 256
ROW_MODES = 16
COL_MODES = 16
H = 2048
W = 2048
MODES = 512
N_ROWS = 16


def block_levels(key, dims, cuts, least, top_value):
    level, own = 1.0, jax.random.fold_in(key, 6)
    for dim, shards_of in cuts:
        steps = jnp.exp(jax.random.uniform(jax.random.fold_in(own, dim), (shards_of,), jnp.float32, least / len(cuts), top_value / len(cuts)))
        level = level * jnp.repeat(steps, dims[dim] // shards_of).reshape([-1 if axis == dim else 1 for axis in range(len(dims))])
    return level


def noise(rng, dims, scale, bound, split=(), kind=jnp.bfloat16):
    drawn = jax.random.normal(rng, dims, jnp.float32) * scale
    if len(split) > 0:
        drawn = block_levels(rng, dims, split, -0.22, 0.18) * drawn
    return jnp.clip(drawn, min=-bound, max=bound).astype(kind)


def setup_inputs(seed: int = 0) -> dict:
    arg_keys = jax.random.split(jax.random.key(seed), 8)
    fine_input = noise(arg_keys[0], (H, W, C), 1.0, 6.0, ((0, 16), (1, 8)))
    cotangent = noise(arg_keys[1], (H, W, C), 1.0, 6.0, ((0, 16), (1, 8)))
    lift_weight = noise(arg_keys[2], (C, CC), (C // 16) ** -0.5, 3.0)
    spectral_weight = noise(arg_keys[3], (2, MODES, CC, CC), 1.0, 6.0, ((1, 128),))
    skip_weight = noise(arg_keys[4], (CC, CC), CC ** -0.5, 0.375)
    down_weight = noise(arg_keys[5], (CC, C), CC ** -0.5, 0.375)
    skip_fine = noise(arg_keys[6], (C, C), C ** -0.5, 0.75)
    return {"fine_input": fine_input, "cotangent": cotangent, "lift_weight": lift_weight, "spectral_weight": spectral_weight, "skip_weight": skip_weight, "down_weight": down_weight, "skip_fine": skip_fine}


highest = lax.Precision.HIGHEST

def row_frequency():
    counter = jnp.arange(2 * ROW_MODES, dtype=jnp.int32)
    return jnp.where(counter < ROW_MODES, counter, counter - 2 * ROW_MODES)

def col_frequency():
    return jnp.arange(COL_MODES, dtype=jnp.int32)

def phase_table(frequency, start, count, period):
    position = start + jnp.arange(count, dtype=jnp.int32)
    phases = jnp.mod(frequency[:, None] * position[None, :], period)
    angles = phases.astype(jnp.float32) * (2.0 * math.pi / period)
    return (jnp.cos(angles), jnp.sin(angles))

def mode_weights(period_rows, period_cols):
    counter = jnp.arange(2 * ROW_MODES * COL_MODES, dtype=jnp.int32)
    doubled = jnp.where(jnp.mod(counter, COL_MODES) == 0, 1.0, 2.0).astype(jnp.float32)
    return doubled / float(period_rows * period_cols)

def analysis(grid_values, row_start, col_start, period_rows, period_cols):
    row_count, col_count, channels = grid_values.shape
    cos_rows, sin_rows = phase_table(row_frequency(), row_start, row_count, period_rows)
    cos_cols, sin_cols = phase_table(col_frequency(), col_start, col_count, period_cols)
    along_real = jnp.einsum('gm,nmi->ngi', cos_cols, grid_values, precision=highest)
    along_imag = -jnp.einsum('gm,nmi->ngi', sin_cols, grid_values, precision=highest)
    real_part = jnp.einsum('jn,ngi->jgi', cos_rows, along_real, precision=highest) + jnp.einsum('jn,ngi->jgi', sin_rows, along_imag, precision=highest)
    imag_part = jnp.einsum('jn,ngi->jgi', cos_rows, along_imag, precision=highest) - jnp.einsum('jn,ngi->jgi', sin_rows, along_real, precision=highest)
    return jnp.stack([real_part, imag_part]).reshape(2, 2 * ROW_MODES * COL_MODES, channels)

def synthesis(spectrum_real, spectrum_imag, row_start, col_start, row_count, col_count, period_rows, period_cols):
    channels = spectrum_real.shape[-1]
    real_grid = spectrum_real.reshape(2 * ROW_MODES, COL_MODES, channels)
    imag_grid = spectrum_imag.reshape(2 * ROW_MODES, COL_MODES, channels)
    cos_rows, sin_rows = phase_table(row_frequency(), row_start, row_count, period_rows)
    cos_cols, sin_cols = phase_table(col_frequency(), col_start, col_count, period_cols)
    turned_real = jnp.einsum('jn,jgo->ngo', cos_rows, real_grid, precision=highest) - jnp.einsum('jn,jgo->ngo', sin_rows, imag_grid, precision=highest)
    turned_imag = jnp.einsum('jn,jgo->ngo', sin_rows, real_grid, precision=highest) + jnp.einsum('jn,jgo->ngo', cos_rows, imag_grid, precision=highest)
    return jnp.einsum('gm,ngo->nmo', cos_cols, turned_real, precision=highest) - jnp.einsum('gm,ngo->nmo', sin_cols, turned_imag, precision=highest)

def mix_modes(spectrum, kernel):
    kernel_real = kernel[0].astype(jnp.float32)
    kernel_imag = kernel[1].astype(jnp.float32)
    out_real = jnp.einsum('mi,mio->mo', spectrum[0], kernel_real, precision=highest) - jnp.einsum('mi,mio->mo', spectrum[1], kernel_imag, precision=highest)
    out_imag = jnp.einsum('mi,mio->mo', spectrum[0], kernel_imag, precision=highest) + jnp.einsum('mi,mio->mo', spectrum[1], kernel_real, precision=highest)
    return jnp.stack([out_real, out_imag])

def spectral_adjoint(spectrum, pulled, kernel):
    kernel_real = kernel[0].astype(jnp.float32)
    kernel_imag = kernel[1].astype(jnp.float32)
    grad_real = jnp.einsum('mi,mo->mio', spectrum[0], pulled[0], precision=highest) + jnp.einsum('mi,mo->mio', spectrum[1], pulled[1], precision=highest)
    grad_imag = jnp.einsum('mi,mo->mio', spectrum[0], pulled[1], precision=highest) - jnp.einsum('mi,mo->mio', spectrum[1], pulled[0], precision=highest)
    back_real = jnp.einsum('mio,mo->mi', kernel_real, pulled[0], precision=highest) + jnp.einsum('mio,mo->mi', kernel_imag, pulled[1], precision=highest)
    back_imag = jnp.einsum('mio,mo->mi', kernel_real, pulled[1], precision=highest) - jnp.einsum('mio,mo->mi', kernel_imag, pulled[0], precision=highest)
    return (jnp.stack([grad_real, grad_imag]), jnp.stack([back_real, back_imag]))

def block_sum(block):
    row_count, col_count, channels = block.shape
    return block.astype(jnp.float32).reshape(row_count // 4, 4, col_count // 4, 4, channels).sum(axis=(1, 3))

def expand(coarse_values):
    return jnp.repeat(jnp.repeat(coarse_values, 4, axis=0), 4, axis=1)

def lift_coarse(block, lift_weight):
    pooled = (block_sum(block) * (1.0 / 16.0)).astype(jnp.bfloat16)
    row_count, col_count, channels = pooled.shape
    coarse = jnp.dot(pooled.reshape(-1, channels), lift_weight, preferred_element_type=jnp.float32).astype(jnp.bfloat16)
    return (pooled, coarse.reshape(row_count, col_count, -1))

def activation_pull(coarse, upstream, skip_weight, down_weight, mixed, weights, row_start, col_start, period_rows, period_cols):
    row_count, col_count, coarse_width = coarse.shape
    coarse_flat = coarse.reshape(-1, coarse_width)
    spectral = synthesis(weights[:, None] * mixed[0], weights[:, None] * mixed[1], row_start, col_start, row_count, col_count, period_rows, period_cols)
    hidden_pre = spectral.reshape(-1, coarse_width) + jnp.dot(coarse_flat, skip_weight, preferred_element_type=jnp.float32)
    activated, pullback = jax.vjp(jax.nn.gelu, hidden_pre)
    summed = block_sum(upstream).astype(jnp.bfloat16)
    summed = summed.reshape(-1, summed.shape[-1])
    pulled_down = jnp.dot(summed, down_weight.T, preferred_element_type=jnp.float32)
    hidden_grad = pullback(pulled_down)[0].astype(jnp.bfloat16)
    return (activated.astype(jnp.bfloat16), summed, hidden_grad)

def reference(fine_input, cotangent, lift_weight, spectral_weight, skip_weight, down_weight, skip_fine):
    grid_rows, grid_cols, channels = fine_input.shape
    coarse_width = lift_weight.shape[1]
    coarse_rows = grid_rows // 4
    coarse_cols = grid_cols // 4
    period_rows = coarse_rows + coarse_rows // 8
    period_cols = coarse_cols + coarse_cols // 8
    slab_rows = grid_rows // N_ROWS
    slab_coarse = slab_rows // 4
    weights = mode_weights(period_rows, period_cols)
    blocks = jnp.arange(N_ROWS, dtype=jnp.int32)
    mode_count = 2 * ROW_MODES * COL_MODES

    def slab_of(array, block_index):
        return lax.dynamic_slice_in_dim(array, (block_index * slab_rows).astype(jnp.int32), slab_rows, 0)

    def first_pass(total, block_index):
        pooled, coarse = lift_coarse(slab_of(fine_input, block_index), lift_weight)
        return (total + analysis(coarse.astype(jnp.float32), block_index * slab_coarse, 0, period_rows, period_cols), None)
    spectrum = lax.scan(first_pass, jnp.zeros((2, mode_count, coarse_width), jnp.float32), blocks)[0]
    mixed = mix_modes(spectrum, spectral_weight)

    def second_pass(totals, block_index):
        input_block = slab_of(fine_input, block_index)
        upstream = slab_of(cotangent, block_index)
        pooled, coarse = lift_coarse(input_block, lift_weight)
        activated, summed, hidden_grad = activation_pull(coarse, upstream, skip_weight, down_weight, mixed, weights, block_index * slab_coarse, 0, period_rows, period_cols)
        coarse_flat = coarse.reshape(-1, coarse_width)
        pulled = analysis(hidden_grad.astype(jnp.float32).reshape(slab_coarse, coarse_cols, coarse_width), block_index * slab_coarse, 0, period_rows, period_cols) * weights[None, :, None]
        input_flat = input_block.reshape(-1, channels)
        upstream_flat = upstream.reshape(-1, channels)
        return ((totals[0] + pulled, totals[1] + jnp.dot(activated.T, summed, preferred_element_type=jnp.float32), totals[2] + jnp.dot(coarse_flat.T, hidden_grad, preferred_element_type=jnp.float32), totals[3] + jnp.dot(input_flat.T, upstream_flat, preferred_element_type=jnp.float32)), None)
    start = (jnp.zeros((2, mode_count, coarse_width), jnp.float32), jnp.zeros((coarse_width, channels), jnp.float32), jnp.zeros((coarse_width, coarse_width), jnp.float32), jnp.zeros((channels, channels), jnp.float32))
    pulled, down_grad, skip_grad, fine_grad = lax.scan(second_pass, start, blocks)[0]
    grad_spectral, back = spectral_adjoint(spectrum, pulled, spectral_weight)

    def third_pass(total, block_index):
        input_block = slab_of(fine_input, block_index)
        upstream = slab_of(cotangent, block_index)
        pooled, coarse = lift_coarse(input_block, lift_weight)
        activated, summed, hidden_grad = activation_pull(coarse, upstream, skip_weight, down_weight, mixed, weights, block_index * slab_coarse, 0, period_rows, period_cols)
        spectral_back = synthesis(back[0], back[1], block_index * slab_coarse, 0, slab_coarse, coarse_cols, period_rows, period_cols)
        coarse_grad = (spectral_back.reshape(-1, coarse_width) + jnp.dot(hidden_grad, skip_weight.T, preferred_element_type=jnp.float32)).astype(jnp.bfloat16)
        lift_term = jnp.dot(pooled.reshape(-1, channels).T, coarse_grad, preferred_element_type=jnp.float32)
        pooled_grad = jnp.dot(coarse_grad, lift_weight.T, preferred_element_type=jnp.float32).reshape(slab_coarse, coarse_cols, channels)
        fine_term = jnp.dot(upstream.reshape(-1, channels), skip_fine.T, preferred_element_type=jnp.float32)
        grad_block = (fine_term.reshape(slab_rows, grid_cols, channels) + expand(pooled_grad) * (1.0 / 16.0)).astype(jnp.bfloat16)
        return (total + lift_term, grad_block)
    lift_grad, grad_blocks = lax.scan(third_pass, jnp.zeros((channels, coarse_width), jnp.float32), blocks)
    grad_input = grad_blocks.reshape(grid_rows, grid_cols, channels)
    coarse_scale = 1.0 / math.sqrt(coarse_rows * coarse_cols)
    fine_scale = 1.0 / math.sqrt(16 * coarse_rows * coarse_cols)
    return (grad_input, grad_spectral, lift_grad * coarse_scale, skip_grad * coarse_scale, down_grad * coarse_scale, fine_grad * fine_scale)
```

```python
import math

import jax
import jax.numpy as jnp
import numpy as np
from jax import lax
from jax.experimental import pallas as pl
from jax.experimental.pallas import tpu as pltpu
from jax.sharding import Mesh, PartitionSpec as P

F32 = jnp.float32
BF16 = jnp.bfloat16
HIGH = lax.Precision.HIGHEST

ROWS = ("z", "xl", "core")
COLS = ("y", "xh")
ALL = ROWS + COLS
SAME_CORE = ("z", "xl", "y", "xh")

PERIOD = 576
N_R, N_C = 16, 8
LR, LC = 32, 64
VMEM = 20 * 1024 * 1024


def _split(table):
    high = table.astype(BF16)
    low = (table - high.astype(np.float64)).astype(BF16)
    return high, low


def _row_tables():
    j = np.arange(32)
    f = np.where(j < 16, j, j - 32)
    n = np.arange(N_R * LR)
    angle = 2.0 * np.pi * np.mod(f[:, None] * n[None, :], PERIOD) / PERIOD
    cos = np.cos(angle).reshape(32, N_R, LR)
    sin = np.sin(angle).reshape(32, N_R, LR)
    m = np.stack([np.stack([cos, sin], -1), np.stack([-sin, cos], -1)], 0)
    m = m.transpose(2, 1, 0, 3, 4)
    full = np.einsum("rjpnq,ts->rjptnqs", m, np.eye(4))
    natural = full.transpose(0, 2, 1, 3, 4, 5, 6).reshape(N_R, 256, 256)
    split = full.reshape(N_R, 8, 2, 2, 2, 4, 256)
    split = split.transpose(0, 2, 1, 3, 4, 5, 6)
    by_core = np.stack([split[r, [r & 1, 1 - (r & 1)]] for r in range(N_R)])
    by_core = by_core.reshape(N_R, 256, 256)
    return tuple(
        np.concatenate(_split(a), -1) for a in (natural, by_core.transpose(0, 2, 1), by_core)
    )


def _col_tables():
    g = np.arange(16)
    m = np.arange(N_C * LC)
    angle = 2.0 * np.pi * np.mod(g[:, None] * m[None, :], PERIOD) / PERIOD
    both = np.stack([np.cos(angle), -np.sin(angle)], 0).reshape(2, 4, 4, N_C, LC)
    table = both.transpose(3, 1, 0, 2, 4).reshape(N_C, 32, LC)
    high, low = _split(table)
    down = np.concatenate([high, low], 1)
    up = np.concatenate([high, low, high], 1).transpose(0, 2, 1)
    wide_high, wide_low = (np.repeat(a, 4, axis=2) for a in _split(table / 16.0))
    spread = np.repeat(np.eye(LC), 4, axis=1) / 16.0
    spread = np.broadcast_to(spread.astype(BF16), (N_C, LC, 4 * LC))
    fine = np.concatenate([wide_high, wide_low, wide_high, spread], 1)
    return down, up, fine


def _dot(a, b, contract=((1,), (0,)), precision=None):
    return lax.dot_general(a, b, (contract, ((), ())), precision=precision, preferred_element_type=F32)


def _dot_nt(a, b, precision=None):
    return _dot(a, b, ((1,), (1,)), precision)


def _halves(a):
    high = a.astype(BF16)
    return high, (a - high.astype(F32)).astype(BF16)


def _turn(table, data):
    high, low = _halves(data)
    return _dot(table, jnp.concatenate([high, high], 0)) + _dot(table[:, :256], low)


def _mode_weight(place_ref):
    row = lax.broadcasted_iota(jnp.int32, (8, 256), 0)
    first = jnp.logical_and(lax.rem(row, 4) == 0, lax.rem(place_ref[1], 4) == 0)
    return jnp.where(first, 1.0, 2.0) * (1.0 / (PERIOD * PERIOD))


def _pool_matrix():
    row = lax.broadcasted_iota(jnp.int32, (512, 64), 0)
    col = lax.broadcasted_iota(jnp.int32, (512, 64), 1)
    return jnp.where(lax.rem(row, 256) // 4 == col, 1.0, 0.0).astype(BF16)


def _sum_blocks(ref, i, pool):
    rows = ref[pl.ds(i * 16, 16)].astype(F32).reshape(4, 4, 64, 256).sum(1).reshape(256, 256)
    return _dot(jnp.concatenate(_halves(rows), 1), pool)


def _pool_kernel(
    place_ref, x_any, natural_any, down_any, up_any, wide_any, syn_any, ana_any,
    p_ref, ps_ref, pst_ref, down_ref, up_ref, wide_ref, syn_ref, ana_ref, x_ref,
    rows_ref, c_ref, x_sem, sem,
):
    r, c = place_ref[0], place_ref[1]
    first = pltpu.make_async_copy(down_any.at[c], down_ref, sem.at[0])
    first.start()
    chunks = [
        pltpu.make_async_copy(x_any.at[pl.ds(32 * k, 32)], x_ref.at[pl.ds(32 * k, 32)], x_sem.at[k])
        for k in range(4)
    ]
    for chunk in chunks:
        chunk.start()
    rest = [
        pltpu.make_async_copy(source.at[at], target, sem.at[k + 1])
        for k, (source, at, target) in enumerate(
            [
                (natural_any, r, rows_ref),
                (up_any, c, up_ref),
                (wide_any, c, wide_ref),
                (syn_any, r, syn_ref),
                (ana_any, r, ana_ref),
            ]
        )
    ]
    for copy in rest:
        copy.start()
    pool = _pool_matrix()
    first.wait()
    down = down_ref[...]
    def narrow(i, xp):
        for n in range(4):
            wide = jnp.concatenate([xp[n], xp[n]], 0).astype(F32).T.astype(BF16)
            ps_ref[i * 4 + n] = wide
            modes = _dot(down, wide)
            modes = modes[:32] + modes[32:]
            at = (i * 4 + n) * 8
            for g in range(4):
                c_ref[g, at : at + 8, :] = modes[g * 8 : (g + 1) * 8]

    held = None
    for i in range(8):
        if i % 2 == 0:
            chunks[i // 2].wait()
        xp = (_sum_blocks(x_ref, i, pool) * (1.0 / 16.0)).astype(BF16)
        xp = [xp[64 * n : 64 * n + 64] for n in range(4)]
        pst_ref[:, 256 * i : 256 * (i + 1)] = jnp.concatenate(xp, 1)
        if held is not None:
            narrow(i - 1, held)
        held = xp
    narrow(7, held)
    for copy in rest:
        copy.wait()
    first_half = lax.broadcasted_iota(jnp.int32, (128, 128), 1) < 64
    for g in range(4):
        done = _turn(rows_ref[...], c_ref[g])
        done = jnp.where(first_half, done[:128], done[128:])
        p_ref[:, g] = done.reshape(32, 4, 128)


def pool_call(place, *operands):
    vm = pl.BlockSpec(memory_space=pltpu.VMEM)
    operands = [pltpu.with_memory_space_constraint(jnp.asarray(a), pltpu.HBM) for a in operands]
    return pl.pallas_call(
        _pool_kernel,
        in_specs=[pl.BlockSpec(memory_space=pltpu.SMEM)] + [pl.BlockSpec(memory_space=pltpu.HBM)] * 7,
        out_specs=[vm] * 9,
        out_shape=[
            jax.ShapeDtypeStruct((32, 4, 4, 128), F32),
            jax.ShapeDtypeStruct((32, 64, 128), BF16),
            jax.ShapeDtypeStruct((64, 2048), BF16),
            jax.ShapeDtypeStruct((64, 64), BF16),
            jax.ShapeDtypeStruct((64, 96), BF16),
            jax.ShapeDtypeStruct((160, 256), BF16),
            jax.ShapeDtypeStruct((256, 512), BF16),
            jax.ShapeDtypeStruct((256, 512), BF16),
            jax.ShapeDtypeStruct((128, 64, 256), BF16),
        ],
        scratch_shapes=[
            pltpu.VMEM((256, 512), BF16),
            pltpu.VMEM((4, 256, 128), F32),
            pltpu.SemaphoreType.DMA((4,)),
            pltpu.SemaphoreType.DMA((6,)),
        ],
        compiler_params=pltpu.CompilerParams(vmem_limit_bytes=VMEM),
        name="pool",
    )(place, *operands)


def _upstream_kernel(x_ref, u_ref, su_ref, sut_ref, fine_ref):
    pool = _pool_matrix()
    term = jnp.zeros((64, 64), F32)
    for i in range(8):
        us = _sum_blocks(u_ref, i, pool).astype(BF16)
        us = [us[64 * n : 64 * n + 64] for n in range(4)]
        sut_ref[:, 256 * i : 256 * (i + 1)] = jnp.concatenate(us, 1)
        for n in range(4):
            su_ref[i * 4 + n] = us[n].astype(F32).T.astype(BF16)
        x_all = jnp.concatenate([x_ref[i * 16 + a] for a in range(16)], 1)
        u_all = jnp.concatenate([u_ref[i * 16 + a] for a in range(16)], 1)
        term += _dot_nt(x_all, u_all)
    fine_ref[...] = term


def upstream_call(x, u):
    vm = pl.BlockSpec(memory_space=pltpu.VMEM)
    return pl.pallas_call(
        _upstream_kernel,
        in_specs=[vm] * 2,
        out_specs=[vm] * 3,
        out_shape=[
            jax.ShapeDtypeStruct((32, 64, 64), BF16),
            jax.ShapeDtypeStruct((64, 2048), BF16),
            jax.ShapeDtypeStruct((64, 64), F32),
        ],
        compiler_params=pltpu.CompilerParams(vmem_limit_bytes=VMEM),
        name="upstream",
    )(x, u)


def _mix_kernel(place_ref, got_ref, lift_ref, w_ref, mixed_ref, p_ref, s_ref):
    p = got_ref[...].sum(0)
    p = jnp.concatenate([p[:, :64], p[:, 64:]], 0)
    p_ref[...] = p
    s = _dot(jnp.concatenate(_halves(p), 0), lift_ref[...])
    s = s[:8] + s[8:]
    s_ref[...] = s
    parts = jnp.concatenate(_halves(s), 0)
    row = lax.broadcasted_iota(jnp.int32, (8, 256), 0)
    sign = jnp.where(row < 4, -1.0, 1.0)
    total = jnp.zeros((8, 256), F32)
    for t in range(4):
        a = _dot(parts, w_ref[0, t])
        b = _dot(parts, w_ref[1, t])
        a = a[:8] + a[8:]
        b = b[:8] + b[8:]
        b = jnp.concatenate([b[4:], b[:4]], 0)
        total = jnp.where(lax.rem(row, 4) == t, a + sign * b, total)
    mixed_ref[...] = jnp.broadcast_to((total * _mode_weight(place_ref))[None], (64, 8, 256))


def mix_call(place, got, lift, weight):
    vm = pl.BlockSpec(memory_space=pltpu.VMEM)
    return pl.pallas_call(
        _mix_kernel,
        in_specs=[pl.BlockSpec(memory_space=pltpu.SMEM), vm, vm, vm],
        out_specs=[vm] * 3,
        out_shape=[
            jax.ShapeDtypeStruct((64, 8, 256), F32),
            jax.ShapeDtypeStruct((8, 64), F32),
            jax.ShapeDtypeStruct((8, 256), F32),
        ],
        compiler_params=pltpu.CompilerParams(vmem_limit_bytes=VMEM),
        name="mix",
    )(place, got, lift, weight)


def _hidden_kernel(
    place_ref, mine_ref, other_ref, ps_ref, pst_ref, su_ref, sut_ref, lift_ref, skip_ref, downt_ref, fine_ref,
    syn_ref, ana_ref, up_ref, down_ref, keep_ref, send_ref, hl_ref, t_ref, c_ref, q_ref, d_ref,
):
    for g in range(4):
        modes = jnp.concatenate([mine_ref[:, g].reshape(128, 256), other_ref[:, g].reshape(128, 256)], 0)
        turned = _turn(syn_ref[...], modes)
        t_ref[:, g * 8 : (g + 1) * 8, :] = turned.reshape(32, 8, 256)
    both = _dot(lift_ref[...], skip_ref[...])
    high, low = _halves(both)
    right = jnp.concatenate([high, low], 0)
    downt = downt_ref[...]
    q_ref[...] = jnp.zeros((64, 256), F32)
    d_ref[...] = jnp.zeros((64, 256), F32)
    root = math.sqrt(2.0 / math.pi)

    def group(i, carry):
        first = _dot(ps_ref[pl.ds(i * 4, 4)].reshape(256, 128), right)
        pulled = _dot(su_ref[pl.ds(i * 4, 4)].reshape(256, 64), downt)
        field = []
        for n in range(4):
            th, tl = _halves(t_ref[i * 4 + n])
            field.append(_dot(up_ref[...], jnp.concatenate([th, th, tl], 0)))
        v = first + jnp.concatenate(field, 0)
        v2 = v * v
        half = 0.5 + 0.5 * jnp.tanh(v * (root + (root * 0.044715) * v2))
        act = (v * half).astype(BF16)
        slope = half * (1.0 + v * (2.0 * root + (6.0 * root * 0.044715) * v2) * (1.0 - half))
        hg = (pulled * slope).astype(BF16)
        lanes = pl.ds(pl.multiple_of(i * 256, 256), 256)
        q_ref[...] += _dot(pst_ref[:, lanes], hg)
        d_ref[...] += _dot(sut_ref[:, lanes], act)
        for n in range(4):
            modes = _dot(down_ref[...], hg[n * 64 : (n + 1) * 64])
            modes = modes[:32] + modes[32:]
            at = pl.multiple_of((i * 4 + n) * 8, 8)
            for g in range(4):
                c_ref[g, pl.ds(at, 8), :] = modes[g * 8 : (g + 1) * 8]
        hl_ref[:, lanes] = _dot_nt(high, hg).astype(BF16)
        return carry

    lax.fori_loop(0, 8, group, 0, unroll=8)
    for g in range(4):
        done = _turn(ana_ref[...], c_ref[g])
        keep_ref[:, g, :, 0:256] = done[:128].reshape(16, 8, 256)
        send_ref[:, g, :, 0:256] = done[128:].reshape(16, 8, 256)
    core = place_ref[2]
    blank = jnp.zeros((64, 64), F32)

    def extras(ref, low_half):
        ref[:, :, :, 256:384] = jnp.zeros((16, 4, 8, 128), F32)
        q = jnp.where(low_half, q_ref[:, 0:128], q_ref[:, 128:256])
        d = jnp.where(low_half, d_ref[:, 0:128], d_ref[:, 128:256])
        planes = [q[:, :64], q[:, 64:], d[:, :64], d[:, 64:], fine_ref[...]]
        for k, plane in enumerate(planes):
            ref[:, :, k, 256:384] = jnp.concatenate([blank, plane], 1).reshape(16, 4, 128)

    extras(keep_ref, core == 0)
    extras(send_ref, core == 1)


def hidden_call(place, *operands):
    vm = pl.BlockSpec(memory_space=pltpu.VMEM)
    return pl.pallas_call(
        _hidden_kernel,
        in_specs=[pl.BlockSpec(memory_space=pltpu.SMEM)] + [vm] * 14,
        out_specs=[vm] * 3,
        out_shape=[
            jax.ShapeDtypeStruct((16, 4, 8, 384), F32),
            jax.ShapeDtypeStruct((16, 4, 8, 384), F32),
            jax.ShapeDtypeStruct((64, 2048), BF16),
        ],
        scratch_shapes=[
            pltpu.VMEM((32, 32, 256), F32),
            pltpu.VMEM((4, 256, 256), F32),
            pltpu.VMEM((64, 256), F32),
            pltpu.VMEM((64, 256), F32),
        ],
        compiler_params=pltpu.CompilerParams(vmem_limit_bytes=VMEM),
        name="hidden",
    )(place, *operands)


def _adjoint_kernel(place_ref, got_ref, p_ref, w_ref, pulled_ref, block_ref):
    total = got_ref[...].sum(0)
    pulled = total[:, :256] * _mode_weight(place_ref)
    pulled_ref[...] = pulled
    parts = jnp.concatenate(_halves(pulled), 0)
    row = lax.broadcasted_iota(jnp.int32, (8, 256), 0)
    sign = jnp.where(row < 4, 1.0, -1.0)
    back = jnp.zeros((8, 256), F32)
    for t in range(4):
        a = _dot_nt(parts, w_ref[0, t])
        b = _dot_nt(parts, w_ref[1, t])
        a = a[:8] + a[8:]
        b = b[:8] + b[8:]
        b = jnp.concatenate([b[4:], b[:4]], 0)
        back = jnp.where(lax.rem(row, 4) == t, a + sign * b, back)
    block = jnp.concatenate([back, p_ref[...], total[:, 320:384]], 1)
    block_ref[...] = jnp.broadcast_to(block[None], (64, 8, 384))


def adjoint_call(place, got, p, weight):
    vm = pl.BlockSpec(memory_space=pltpu.VMEM)
    return pl.pallas_call(
        _adjoint_kernel,
        in_specs=[pl.BlockSpec(memory_space=pltpu.SMEM)] + [vm] * 3,
        out_specs=[vm] * 2,
        out_shape=[
            jax.ShapeDtypeStruct((8, 256), F32),
            jax.ShapeDtypeStruct((64, 8, 384), F32),
        ],
        compiler_params=pltpu.CompilerParams(vmem_limit_bytes=VMEM),
        name="adjoint",
    )(place, got, p, weight)


def _gathered(ref, lift):
    high, low = _halves(ref[:, :, :, 0:256].reshape(512, 256))
    narrow = _dot_nt(high, lift) + _dot_nt(low, lift)
    p_high, p_low = _halves(ref[:, :, :, 256:384].reshape(512, 128).T[:64])
    both = _dot(jnp.concatenate([p_high, p_low], 0), high)
    return narrow, both[:64] + both[64:] + _dot(p_high, low)


def _outer_kernel(s_ref, pulled_ref, mine_ref, lift_ref, grad_any, narrow_ref, sum_ref, grad_ref, sem):
    s = s_ref[...].T
    pulled = pulled_ref[...]
    copies = []
    for t in range(4):
        s0, s1 = s[:, t : t + 1], s[:, 4 + t : 5 + t]
        p0, p1 = pulled[t : t + 1], pulled[4 + t : 5 + t]
        grad_ref[0, t] = s0 * p0 + s1 * p1
        grad_ref[1, t] = s0 * p1 - s1 * p0
        for part in range(2):
            copies.append(pltpu.make_async_copy(grad_ref.at[part, t], grad_any.at[part, t], sem.at[part, t]))
            copies[-1].start()
    narrow_ref[...], sum_ref[...] = _gathered(mine_ref, lift_ref[...])
    for copy in copies:
        copy.wait()


def outer_call(s, pulled, mine, lift):
    vm = pl.BlockSpec(memory_space=pltpu.VMEM)
    return pl.pallas_call(
        _outer_kernel,
        in_specs=[vm] * 4,
        out_specs=[pl.BlockSpec(memory_space=pl.ANY), vm, vm],
        out_shape=[
            jax.ShapeDtypeStruct((2, 4, 256, 256), F32),
            jax.ShapeDtypeStruct((512, 64), F32),
            jax.ShapeDtypeStruct((64, 256), F32),
        ],
        scratch_shapes=[pltpu.VMEM((2, 4, 256, 256), F32), pltpu.SemaphoreType.DMA((2, 4))],
        compiler_params=pltpu.CompilerParams(vmem_limit_bytes=VMEM),
        cost_estimate=pl.CostEstimate(flops=2_000_000, bytes_accessed=2_200_000, transcendentals=0),
        name="outer",
    )(s, pulled, mine, lift)


def _term_kernel(u_ref, sf_ref, out_ref):
    row = lax.broadcasted_iota(jnp.int32, (256, 256), 0)
    col = lax.broadcasted_iota(jnp.int32, (256, 256), 1)
    sf = sf_ref[...].astype(F32)
    sf = jnp.concatenate([jnp.concatenate([sf] * 4, 1)] * 4, 0)
    sf = jnp.where(row // 64 == col // 64, sf, 0.0).astype(BF16)
    for n in range(32):
        out_ref[4 * n : 4 * n + 4] = _dot(sf, u_ref[4 * n : 4 * n + 4].reshape(256, 256)).reshape(4, 64, 256)


def term_call(u, sf):
    vm = pl.BlockSpec(memory_space=pltpu.VMEM)
    return pl.pallas_call(
        _term_kernel,
        in_specs=[vm] * 2,
        out_specs=vm,
        out_shape=jax.ShapeDtypeStruct((128, 64, 256), F32),
        compiler_params=pltpu.CompilerParams(vmem_limit_bytes=VMEM),
        cost_estimate=pl.CostEstimate(flops=400_000_000, bytes_accessed=12_000_000, transcendentals=0),
        name="term",
    )(u, sf)


def _fine_kernel(
    place_ref, term_ref, hl_ref, mine_ref, narrow_ref, sum_ref, other_ref, lift_ref, skip_ref, syn_ref, wide_ref,
    out_any, lift_out, skip_out, down_out, fine_out, t_ref, out_ref, sem,
):
    lift = lift_ref[...]
    far_narrow, far_sum = _gathered(other_ref, lift)
    narrow = [a.reshape(16, 4, 8, 64) for a in (narrow_ref[...], far_narrow)]
    for g in range(4):
        modes = jnp.concatenate([half[:, g].reshape(128, 64) for half in narrow], 0)
        t_ref[:, g * 8 : (g + 1) * 8, :] = _turn(syn_ref[...], modes).reshape(32, 8, 64)

    def chunk_copy(i):
        at = pl.ds(i * 16, 16)
        return pltpu.make_async_copy(out_ref.at[at], out_any.at[at], sem.at[i])

    def chunk(i, carry):
        hl = hl_ref[:, pl.ds(pl.multiple_of(i * 256, 256), 256)]
        th, tl = _halves(t_ref[pl.ds(i * 4, 4)].reshape(128, 64).T)
        for n in range(4):
            own = slice(32 * n, 32 * n + 32)
            left = jnp.concatenate([th[:, own], th[:, own], tl[:, own], hl[:, n * 64 : (n + 1) * 64]], 1)
            base = _dot(left, wide_ref[...])
            at = pl.ds(i * 16 + 4 * n, 4)
            out_ref[at] = (term_ref[at] + base[None]).astype(BF16)
        chunk_copy(i).start()
        return carry

    lax.fori_loop(0, 8, chunk, 0, unroll=8)
    low_core = place_ref[2] == 0
    scale = 1.0 / 512.0

    def joined(k):
        own = jnp.concatenate([mine_ref[:, :, j, 320:384].reshape(64, 64) for j in (k, k + 1)], 1)
        far = jnp.concatenate([other_ref[:, :, j, 320:384].reshape(64, 64) for j in (k, k + 1)], 1)
        return jnp.where(low_core, jnp.concatenate([own, far], 1), jnp.concatenate([far, own], 1))

    q = joined(0)
    down_out[...] = joined(2) * scale
    fine_out[...] = mine_ref[:, :, 4, 320:384].reshape(64, 64) * (1.0 / 2048.0)
    q_parts = jnp.concatenate(_halves(q), 0)
    tall = lift.astype(F32).T.astype(BF16)
    skip_out[...] = _dot(jnp.concatenate([tall, tall], 1), q_parts) * scale
    lift_sum = _dot_nt(q_parts, skip_ref[...])
    lift_sum = lift_sum[:64] + lift_sum[64:]
    lift_sum += sum_ref[...] + far_sum
    lift_out[...] = lift_sum * scale

    def settle(i, carry):
        chunk_copy(i).wait()
        return carry

    lax.fori_loop(0, 8, settle, 0)


def fine_call(place, *operands):
    vm = pl.BlockSpec(memory_space=pltpu.VMEM)
    return pl.pallas_call(
        _fine_kernel,
        in_specs=[pl.BlockSpec(memory_space=pltpu.SMEM)] + [vm] * 10,
        out_specs=[pl.BlockSpec(memory_space=pl.ANY)] + [vm] * 4,
        out_shape=[
            jax.ShapeDtypeStruct((128, 64, 256), BF16),
            jax.ShapeDtypeStruct((64, 256), F32),
            jax.ShapeDtypeStruct((256, 256), F32),
            jax.ShapeDtypeStruct((64, 256), F32),
            jax.ShapeDtypeStruct((64, 64), F32),
        ],
        scratch_shapes=[
            pltpu.VMEM((32, 32, 64), F32),
            pltpu.VMEM((128, 64, 256), BF16),
            pltpu.SemaphoreType.DMA((8,)),
        ],
        compiler_params=pltpu.CompilerParams(vmem_limit_bytes=VMEM),
        name="fine",
    )(place, *operands)


def other_core(a):
    return lax.ppermute(a, "core", [(0, 1), (1, 0)])


def to_all(copies):
    mine = lax.all_to_all(copies, SAME_CORE, 0, 0, tiled=True)
    mine = mine.reshape(16, 4, 8, -1)
    return mine, other_core(mine)


def body(fine_input, cotangent, lift, weight, skip, down, skip_fine):
    natural, syn_all, ana_all = _row_tables()
    col_down, col_up, col_fine = _col_tables()
    place = jnp.stack([lax.axis_index(ROWS), lax.axis_index(COLS), lax.axis_index("core")]).astype(jnp.int32)
    x = fine_input.transpose(0, 2, 1)
    u = cotangent.transpose(0, 2, 1)
    partial, ps, pst, to_modes, to_grid, to_fine, syn, ana, held = pool_call(
        place, x, natural, col_down, col_up, col_fine, syn_all, ana_all
    )
    got = lax.all_to_all(partial.reshape(128, 4, 128), ALL, 0, 0, tiled=True)
    mixed, p, s = mix_call(place, got, lift, weight)
    mine, other = to_all(mixed)
    su, sut, fine = upstream_call(held, u)
    keep, send, hl = hidden_call(
        place, mine, other, ps, pst, su, sut, lift, skip, down.T, fine, syn, ana, to_grid, to_modes
    )
    far = other_core(send)
    term = term_call(u, skip_fine)
    keep, term = lax.optimization_barrier((keep, term))
    summed = (keep + far).reshape(64, 8, 384)
    got = lax.all_to_all(summed, SAME_CORE, 0, 0, tiled=True)
    pulled, block = adjoint_call(place, got, p, weight)
    mine, other = to_all(block)
    grad_spectral, narrow, lift_sum = outer_call(s, pulled, mine, lift)
    grad_input, g_lift, g_skip, g_down, g_fine = fine_call(
        place, term, hl, mine, narrow, lift_sum, other, lift, skip, syn, to_fine
    )
    return grad_input.transpose(0, 2, 1), grad_spectral, g_lift, g_skip, g_down.T, g_fine


def solution(mesh):
    split = Mesh(mesh.devices.reshape(4, 2, 2, 4, 2), ALL)
    grid = P(ROWS, COLS, None)
    modes = P(None, ALL, None, None)
    return jax.shard_map(
        body,
        mesh=split,
        in_specs=(grid, grid, P(), modes, P(), P(), P()),
        out_specs=(grid, modes, P(), P(), P(), P()),
        check_vma=False,
    )
```

```python
import math

import jax
import jax.numpy as jnp
import numpy as np
from jax import lax
from jax.experimental import pallas as pl
from jax.experimental.pallas import tpu as pltpu
from jax.sharding import Mesh, PartitionSpec as P

F32 = jnp.float32
BF16 = jnp.bfloat16
HIGH = lax.Precision.HIGHEST

ROWS = ("z", "xl", "core")
COLS = ("y", "xh")
ALL = ROWS + COLS
SAME_CORE = COLS + ("z", "xl")

PERIOD = 576
N_R, N_C = 16, 8
LR, LC = 32, 64
VMEM = 20 * 1024 * 1024


def _split(table):
    high = table.astype(BF16)
    low = (table - high.astype(np.float64)).astype(BF16)
    return high, low


def _row_tables():
    j = np.arange(32)
    f = np.where(j < 16, j, j - 32)
    n = np.arange(N_R * LR)
    angle = 2.0 * np.pi * np.mod(f[:, None] * n[None, :], PERIOD) / PERIOD
    cos = np.cos(angle).reshape(32, N_R, LR)
    sin = np.sin(angle).reshape(32, N_R, LR)
    m = np.stack([np.stack([cos, sin], -1), np.stack([-sin, cos], -1)], 0)
    m = m.transpose(2, 1, 0, 3, 4)
    full = np.einsum("rjpnq,ts->rjptnqs", m, np.eye(4))
    natural = full.transpose(0, 2, 1, 3, 4, 5, 6).reshape(N_R, 256, 256)
    split = full.reshape(N_R, 8, 2, 2, 2, 4, 256)
    split = split.transpose(0, 2, 3, 1, 4, 5, 6)
    by_core = np.stack([split[r, [r & 1, 1 - (r & 1)]] for r in range(N_R)])
    by_core = by_core.reshape(N_R, 256, 256)
    return tuple(
        np.concatenate(_split(a), -1) for a in (natural, by_core.transpose(0, 2, 1), by_core)
    )


def _col_tables():
    g = np.arange(16)
    m = np.arange(N_C * LC)
    angle = 2.0 * np.pi * np.mod(g[:, None] * m[None, :], PERIOD) / PERIOD
    both = np.stack([np.cos(angle), -np.sin(angle)], 0).reshape(2, 4, 4, N_C, LC)
    table = both.transpose(3, 1, 0, 2, 4).reshape(N_C, 32, LC)
    high, low = _split(table)
    down = np.concatenate([high, low], 1)
    up = np.concatenate([high, low, high], 1).transpose(0, 2, 1)
    wide_high, wide_low = (np.repeat(a, 4, axis=2) for a in _split(table / 16.0))
    spread = np.repeat(np.eye(LC), 4, axis=1) / 16.0
    spread = np.broadcast_to(spread.astype(BF16), (N_C, LC, 4 * LC))
    fine = np.concatenate([wide_high, wide_low, wide_high, spread], 1)
    return down, up, fine


def _dot(a, b, contract=((1,), (0,)), precision=None):
    return lax.dot_general(a, b, (contract, ((), ())), precision=precision, preferred_element_type=F32)


def _dot_nt(a, b, precision=None):
    return _dot(a, b, ((1,), (1,)), precision)


def _halves(a):
    high = a.astype(BF16)
    return high, (a - high.astype(F32)).astype(BF16)


def _turn(table, data):
    high, low = _halves(data)
    return _dot(table, jnp.concatenate([high, high], 0)) + _dot(table[:, :256], low)


def _mode_weight(place_ref):
    row = lax.broadcasted_iota(jnp.int32, (8, 256), 0)
    first = jnp.logical_and(lax.rem(row, 4) == 0, lax.rem(place_ref[1], 4) == 0)
    return jnp.where(first, 1.0, 2.0) * (1.0 / (PERIOD * PERIOD))


def _pool_matrix():
    row = lax.broadcasted_iota(jnp.int32, (512, 64), 0)
    col = lax.broadcasted_iota(jnp.int32, (512, 64), 1)
    return jnp.where(lax.rem(row, 256) // 4 == col, 1.0, 0.0).astype(BF16)


def _sum_blocks(ref, i, pool):
    rows = ref[pl.ds(i * 16, 16)].astype(F32).reshape(4, 4, 64, 256).sum(1).reshape(256, 256)
    return _dot(jnp.concatenate(_halves(rows), 1), pool)


def _pool_kernel(
    place_ref, x_any, natural_any, down_any, up_any, wide_any, syn_any, ana_any,
    p_ref, ps_ref, pst_ref, down_ref, up_ref, wide_ref, syn_ref, ana_ref, x_ref,
    rows_ref, c_ref, x_sem, sem,
):
    r, c = place_ref[0], place_ref[1]
    first = pltpu.make_async_copy(down_any.at[c], down_ref, sem.at[0])
    first.start()
    chunks = [
        pltpu.make_async_copy(x_any.at[pl.ds(32 * k, 32)], x_ref.at[pl.ds(32 * k, 32)], x_sem.at[k])
        for k in range(4)
    ]
    for chunk in chunks:
        chunk.start()
    rest = [
        pltpu.make_async_copy(source.at[at], target, sem.at[k + 1])
        for k, (source, at, target) in enumerate(
            [
                (natural_any, r, rows_ref),
                (up_any, c, up_ref),
                (wide_any, c, wide_ref),
                (syn_any, r, syn_ref),
                (ana_any, r, ana_ref),
            ]
        )
    ]
    for copy in rest:
        copy.start()
    pool = _pool_matrix()
    first.wait()
    down = down_ref[...]
    def narrow(i, xp):
        for n in range(4):
            wide = jnp.concatenate([xp[n], xp[n]], 0).astype(F32).T.astype(BF16)
            ps_ref[i * 4 + n] = wide
            modes = _dot(down, wide)
            modes = modes[:32] + modes[32:]
            at = (i * 4 + n) * 8
            for g in range(4):
                c_ref[g, at : at + 8, :] = modes[g * 8 : (g + 1) * 8]

    held = None
    for i in range(8):
        if i % 2 == 0:
            chunks[i // 2].wait()
        xp = (_sum_blocks(x_ref, i, pool) * (1.0 / 16.0)).astype(BF16)
        xp = [xp[64 * n : 64 * n + 64] for n in range(4)]
        pst_ref[:, 256 * i : 256 * (i + 1)] = jnp.concatenate(xp, 1)
        if held is not None:
            narrow(i - 1, held)
        held = xp
    narrow(7, held)
    for copy in rest:
        copy.wait()
    first_half = lax.broadcasted_iota(jnp.int32, (128, 128), 1) < 64
    for g in range(4):
        done = _turn(rows_ref[...], c_ref[g])
        done = jnp.where(first_half, done[:128], done[128:])
        p_ref[:, g] = done.reshape(32, 4, 128)


def pool_call(place, *operands):
    vm = pl.BlockSpec(memory_space=pltpu.VMEM)
    operands = [pltpu.with_memory_space_constraint(jnp.asarray(a), pltpu.HBM) for a in operands]
    return pl.pallas_call(
        _pool_kernel,
        in_specs=[pl.BlockSpec(memory_space=pltpu.SMEM)] + [pl.BlockSpec(memory_space=pltpu.HBM)] * 7,
        out_specs=[vm] * 9,
        out_shape=[
            jax.ShapeDtypeStruct((32, 4, 4, 128), F32),
            jax.ShapeDtypeStruct((32, 64, 128), BF16),
            jax.ShapeDtypeStruct((64, 2048), BF16),
            jax.ShapeDtypeStruct((64, 64), BF16),
            jax.ShapeDtypeStruct((64, 96), BF16),
            jax.ShapeDtypeStruct((160, 256), BF16),
            jax.ShapeDtypeStruct((256, 512), BF16),
            jax.ShapeDtypeStruct((256, 512), BF16),
            jax.ShapeDtypeStruct((128, 64, 256), BF16),
        ],
        scratch_shapes=[
            pltpu.VMEM((256, 512), BF16),
            pltpu.VMEM((4, 256, 128), F32),
            pltpu.SemaphoreType.DMA((4,)),
            pltpu.SemaphoreType.DMA((6,)),
        ],
        compiler_params=pltpu.CompilerParams(vmem_limit_bytes=VMEM),
        name="pool",
    )(place, *operands)


def _upstream_kernel(x_ref, u_ref, su_ref, sut_ref, fine_ref):
    pool = _pool_matrix()
    term = jnp.zeros((64, 64), F32)
    for i in range(8):
        us = _sum_blocks(u_ref, i, pool).astype(BF16)
        us = [us[64 * n : 64 * n + 64] for n in range(4)]
        sut_ref[:, 256 * i : 256 * (i + 1)] = jnp.concatenate(us, 1)
        for n in range(4):
            su_ref[i * 4 + n] = us[n].astype(F32).T.astype(BF16)
        x_all = jnp.concatenate([x_ref[i * 16 + a] for a in range(16)], 1)
        u_all = jnp.concatenate([u_ref[i * 16 + a] for a in range(16)], 1)
        term += _dot_nt(x_all, u_all)
    fine_ref[...] = term


def upstream_call(x, u):
    vm = pl.BlockSpec(memory_space=pltpu.VMEM)
    return pl.pallas_call(
        _upstream_kernel,
        in_specs=[vm] * 2,
        out_specs=[vm] * 3,
        out_shape=[
            jax.ShapeDtypeStruct((32, 64, 64), BF16),
            jax.ShapeDtypeStruct((64, 2048), BF16),
            jax.ShapeDtypeStruct((64, 64), F32),
        ],
        compiler_params=pltpu.CompilerParams(vmem_limit_bytes=VMEM),
        name="upstream",
    )(x, u)


def _mix_kernel(place_ref, got_ref, lift_ref, w_ref, mixed_ref, p_ref, s_ref):
    p = got_ref[...].sum(0)
    p = jnp.concatenate([p[:, :64], p[:, 64:]], 0)
    p_ref[...] = p
    s = _dot(jnp.concatenate(_halves(p), 0), lift_ref[...])
    s = s[:8] + s[8:]
    s_ref[...] = s
    parts = jnp.concatenate(_halves(s), 0)
    row = lax.broadcasted_iota(jnp.int32, (8, 256), 0)
    sign = jnp.where(row < 4, -1.0, 1.0)
    total = jnp.zeros((8, 256), F32)
    for t in range(4):
        a = _dot(parts, w_ref[0, t])
        b = _dot(parts, w_ref[1, t])
        a = a[:8] + a[8:]
        b = b[:8] + b[8:]
        b = jnp.concatenate([b[4:], b[:4]], 0)
        total = jnp.where(lax.rem(row, 4) == t, a + sign * b, total)
    mixed_ref[...] = jnp.broadcast_to((total * _mode_weight(place_ref))[None], (64, 8, 256))


def mix_call(place, got, lift, weight):
    vm = pl.BlockSpec(memory_space=pltpu.VMEM)
    return pl.pallas_call(
        _mix_kernel,
        in_specs=[pl.BlockSpec(memory_space=pltpu.SMEM), vm, vm, vm],
        out_specs=[vm] * 3,
        out_shape=[
            jax.ShapeDtypeStruct((64, 8, 256), F32),
            jax.ShapeDtypeStruct((8, 64), F32),
            jax.ShapeDtypeStruct((8, 256), F32),
        ],
        compiler_params=pltpu.CompilerParams(vmem_limit_bytes=VMEM),
        name="mix",
    )(place, got, lift, weight)


def _hidden_kernel(
    place_ref, mine_ref, other_ref, ps_ref, pst_ref, su_ref, sut_ref, lift_ref, skip_ref, downt_ref, fine_ref,
    syn_ref, ana_ref, up_ref, down_ref, keep_ref, send_ref, hl_ref, t_ref, c_ref, q_ref, d_ref,
):
    for g in range(4):
        modes = jnp.concatenate([mine_ref[:, g].reshape(128, 256), other_ref[:, g].reshape(128, 256)], 0)
        turned = _turn(syn_ref[...], modes)
        t_ref[:, g * 8 : (g + 1) * 8, :] = turned.reshape(32, 8, 256)
    both = _dot(lift_ref[...], skip_ref[...])
    high, low = _halves(both)
    right = jnp.concatenate([high, low], 0)
    downt = downt_ref[...]
    q_ref[...] = jnp.zeros((64, 256), F32)
    d_ref[...] = jnp.zeros((64, 256), F32)
    root = math.sqrt(2.0 / math.pi)

    def group(i, carry):
        first = _dot(ps_ref[pl.ds(i * 4, 4)].reshape(256, 128), right)
        pulled = _dot(su_ref[pl.ds(i * 4, 4)].reshape(256, 64), downt)
        field = []
        for n in range(4):
            th, tl = _halves(t_ref[i * 4 + n])
            field.append(_dot(up_ref[...], jnp.concatenate([th, th, tl], 0)))
        v = first + jnp.concatenate(field, 0)
        v2 = v * v
        half = 0.5 + 0.5 * jnp.tanh(v * (root + (root * 0.044715) * v2))
        act = (v * half).astype(BF16)
        slope = half * (1.0 + v * (2.0 * root + (6.0 * root * 0.044715) * v2) * (1.0 - half))
        hg = (pulled * slope).astype(BF16)
        lanes = pl.ds(pl.multiple_of(i * 256, 256), 256)
        q_ref[...] += _dot(pst_ref[:, lanes], hg)
        d_ref[...] += _dot(sut_ref[:, lanes], act)
        for n in range(4):
            modes = _dot(down_ref[...], hg[n * 64 : (n + 1) * 64])
            modes = modes[:32] + modes[32:]
            at = pl.multiple_of((i * 4 + n) * 8, 8)
            for g in range(4):
                c_ref[g, pl.ds(at, 8), :] = modes[g * 8 : (g + 1) * 8]
        hl_ref[:, lanes] = _dot_nt(high, hg).astype(BF16)
        return carry

    lax.fori_loop(0, 8, group, 0, unroll=8)
    for g in range(4):
        done = _turn(ana_ref[...], c_ref[g])
        for ref, mine in ((keep_ref, done[:128]), (send_ref, done[128:])):
            mine = mine.reshape(2, 8, 8, 256)
            for k in range(4):
                lanes, rows = 128 * (k // 2), 4 * (k % 2)
                ref[:, g, :, k] = mine[:, :, rows : rows + 4, lanes : lanes + 128]
    core = place_ref[2]
    fine = jnp.concatenate([fine_ref[...], jnp.zeros((64, 64), F32)], 1)

    def extras(ref, low_half):
        q = jnp.where(low_half, q_ref[:, 0:128], q_ref[:, 128:256])
        d = jnp.where(low_half, d_ref[:, 0:128], d_ref[:, 128:256])
        for k, plane in enumerate((q, d, fine, jnp.zeros((64, 128), F32))):
            ref[:, :, :, 4, k, :] = plane.reshape(2, 4, 8, 128)

    extras(keep_ref, core == 0)
    extras(send_ref, core == 1)


def hidden_call(place, *operands):
    vm = pl.BlockSpec(memory_space=pltpu.VMEM)
    return pl.pallas_call(
        _hidden_kernel,
        in_specs=[pl.BlockSpec(memory_space=pltpu.SMEM)] + [vm] * 14,
        out_specs=[vm] * 3,
        out_shape=[
            jax.ShapeDtypeStruct((2, 4, 8, 5, 4, 128), F32),
            jax.ShapeDtypeStruct((2, 4, 8, 5, 4, 128), F32),
            jax.ShapeDtypeStruct((64, 2048), BF16),
        ],
        scratch_shapes=[
            pltpu.VMEM((32, 32, 256), F32),
            pltpu.VMEM((4, 256, 256), F32),
            pltpu.VMEM((64, 256), F32),
            pltpu.VMEM((64, 256), F32),
        ],
        compiler_params=pltpu.CompilerParams(vmem_limit_bytes=VMEM),
        name="hidden",
    )(place, *operands)


def _adjoint_kernel(place_ref, got_ref, p_ref, w_ref, pulled_ref, block_ref):
    total = got_ref[...].sum(0)
    pulled = jnp.concatenate([jnp.concatenate([total[k], total[k + 1]], 0) for k in (0, 2)], 1)
    pulled = pulled * _mode_weight(place_ref)
    sums = total[4]
    sums = jnp.concatenate(
        [sums[0:1, :64], sums[0:1, 64:], sums[1:2, :64], sums[1:2, 64:], sums[2:3, :64], jnp.zeros((3, 64), F32)], 0
    )
    pulled_ref[...] = pulled
    parts = jnp.concatenate(_halves(pulled), 0)
    row = lax.broadcasted_iota(jnp.int32, (8, 256), 0)
    sign = jnp.where(row < 4, 1.0, -1.0)
    back = jnp.zeros((8, 256), F32)
    for t in range(4):
        a = _dot_nt(parts, w_ref[0, t])
        b = _dot_nt(parts, w_ref[1, t])
        a = a[:8] + a[8:]
        b = b[:8] + b[8:]
        b = jnp.concatenate([b[4:], b[:4]], 0)
        back = jnp.where(lax.rem(row, 4) == t, a + sign * b, back)
    block = jnp.concatenate([back, p_ref[...], sums], 1)
    block_ref[...] = jnp.broadcast_to(block[None], (64, 8, 384))


def adjoint_call(place, got, p, weight):
    vm = pl.BlockSpec(memory_space=pltpu.VMEM)
    return pl.pallas_call(
        _adjoint_kernel,
        in_specs=[pl.BlockSpec(memory_space=pltpu.SMEM)] + [vm] * 3,
        out_specs=[vm] * 2,
        out_shape=[
            jax.ShapeDtypeStruct((8, 256), F32),
            jax.ShapeDtypeStruct((64, 8, 384), F32),
        ],
        compiler_params=pltpu.CompilerParams(vmem_limit_bytes=VMEM),
        name="adjoint",
    )(place, got, p, weight)


def _gathered(ref, lift):
    high, low = _halves(ref[:, :, :, :, 0:256].reshape(512, 256))
    narrow = _dot_nt(high, lift) + _dot_nt(low, lift)
    p_high, p_low = _halves(ref[:, :, :, :, 256:384].reshape(512, 128).T[:64])
    both = _dot(jnp.concatenate([p_high, p_low], 0), high)
    return narrow, both[:64] + both[64:] + _dot(p_high, low)


def _outer_kernel(s_ref, pulled_ref, mine_ref, lift_ref, grad_any, narrow_ref, sum_ref, grad_ref, sem):
    s = s_ref[...].T
    pulled = pulled_ref[...]
    copies = []
    for t in range(4):
        s0, s1 = s[:, t : t + 1], s[:, 4 + t : 5 + t]
        p0, p1 = pulled[t : t + 1], pulled[4 + t : 5 + t]
        grad_ref[0, t] = s0 * p0 + s1 * p1
        grad_ref[1, t] = s0 * p1 - s1 * p0
        for part in range(2):
            copies.append(pltpu.make_async_copy(grad_ref.at[part, t], grad_any.at[part, t], sem.at[part, t]))
            copies[-1].start()
    narrow_ref[...], sum_ref[...] = _gathered(mine_ref, lift_ref[...])
    for copy in copies:
        copy.wait()


def outer_call(s, pulled, mine, lift):
    vm = pl.BlockSpec(memory_space=pltpu.VMEM)
    return pl.pallas_call(
        _outer_kernel,
        in_specs=[vm] * 4,
        out_specs=[pl.BlockSpec(memory_space=pl.ANY), vm, vm],
        out_shape=[
            jax.ShapeDtypeStruct((2, 4, 256, 256), F32),
            jax.ShapeDtypeStruct((512, 64), F32),
            jax.ShapeDtypeStruct((64, 256), F32),
        ],
        scratch_shapes=[pltpu.VMEM((2, 4, 256, 256), F32), pltpu.SemaphoreType.DMA((2, 4))],
        compiler_params=pltpu.CompilerParams(vmem_limit_bytes=VMEM),
        cost_estimate=pl.CostEstimate(flops=2_000_000, bytes_accessed=2_200_000, transcendentals=0),
        name="outer",
    )(s, pulled, mine, lift)


def _term_kernel(u_ref, sf_ref, out_ref):
    row = lax.broadcasted_iota(jnp.int32, (256, 256), 0)
    col = lax.broadcasted_iota(jnp.int32, (256, 256), 1)
    sf = sf_ref[...].astype(F32)
    sf = jnp.concatenate([jnp.concatenate([sf] * 4, 1)] * 4, 0)
    sf = jnp.where(row // 64 == col // 64, sf, 0.0).astype(BF16)
    for n in range(32):
        out_ref[4 * n : 4 * n + 4] = _dot(sf, u_ref[4 * n : 4 * n + 4].reshape(256, 256)).reshape(4, 64, 256)


def term_call(u, sf):
    vm = pl.BlockSpec(memory_space=pltpu.VMEM)
    return pl.pallas_call(
        _term_kernel,
        in_specs=[vm] * 2,
        out_specs=vm,
        out_shape=jax.ShapeDtypeStruct((128, 64, 256), F32),
        compiler_params=pltpu.CompilerParams(vmem_limit_bytes=VMEM),
        cost_estimate=pl.CostEstimate(flops=400_000_000, bytes_accessed=12_000_000, transcendentals=0),
        name="term",
    )(u, sf)


def _fine_kernel(
    place_ref, term_ref, hl_ref, mine_ref, narrow_ref, sum_ref, other_ref, lift_ref, skip_ref, syn_ref, wide_ref,
    out_any, lift_out, skip_out, down_out, fine_out, t_ref, out_ref, sem,
):
    lift = lift_ref[...]
    far_narrow, far_sum = _gathered(other_ref, lift)
    narrow = [a.reshape(2, 4, 8, 8, 64) for a in (narrow_ref[...], far_narrow)]
    for g in range(4):
        modes = jnp.concatenate([half[:, g].reshape(128, 64) for half in narrow], 0)
        t_ref[:, g * 8 : (g + 1) * 8, :] = _turn(syn_ref[...], modes).reshape(32, 8, 64)

    def chunk_copy(i):
        at = pl.ds(i * 16, 16)
        return pltpu.make_async_copy(out_ref.at[at], out_any.at[at], sem.at[i])

    def chunk(i, carry):
        hl = hl_ref[:, pl.ds(pl.multiple_of(i * 256, 256), 256)]
        th, tl = _halves(t_ref[pl.ds(i * 4, 4)].reshape(128, 64).T)
        for n in range(4):
            own = slice(32 * n, 32 * n + 32)
            left = jnp.concatenate([th[:, own], th[:, own], tl[:, own], hl[:, n * 64 : (n + 1) * 64]], 1)
            base = _dot(left, wide_ref[...])
            at = pl.ds(i * 16 + 4 * n, 4)
            out_ref[at] = (term_ref[at] + base[None]).astype(BF16)
        chunk_copy(i).start()
        return carry

    lax.fori_loop(0, 8, chunk, 0, unroll=8)
    low_core = place_ref[2] == 0
    scale = 1.0 / 512.0

    def joined(k):
        own = jnp.concatenate([mine_ref[:, :, :, j, 320:384].reshape(64, 64) for j in (k, k + 1)], 1)
        far = jnp.concatenate([other_ref[:, :, :, j, 320:384].reshape(64, 64) for j in (k, k + 1)], 1)
        return jnp.where(low_core, jnp.concatenate([own, far], 1), jnp.concatenate([far, own], 1))

    q = joined(0)
    down_out[...] = joined(2) * scale
    fine_out[...] = mine_ref[:, :, :, 4, 320:384].reshape(64, 64) * (1.0 / 2048.0)
    q_parts = jnp.concatenate(_halves(q), 0)
    tall = lift.astype(F32).T.astype(BF16)
    skip_out[...] = _dot(jnp.concatenate([tall, tall], 1), q_parts) * scale
    lift_sum = _dot_nt(q_parts, skip_ref[...])
    lift_sum = lift_sum[:64] + lift_sum[64:]
    lift_sum += sum_ref[...] + far_sum
    lift_out[...] = lift_sum * scale

    def settle(i, carry):
        chunk_copy(i).wait()
        return carry

    lax.fori_loop(0, 8, settle, 0)


def fine_call(place, *operands):
    vm = pl.BlockSpec(memory_space=pltpu.VMEM)
    return pl.pallas_call(
        _fine_kernel,
        in_specs=[pl.BlockSpec(memory_space=pltpu.SMEM)] + [vm] * 10,
        out_specs=[pl.BlockSpec(memory_space=pl.ANY)] + [vm] * 4,
        out_shape=[
            jax.ShapeDtypeStruct((128, 64, 256), BF16),
            jax.ShapeDtypeStruct((64, 256), F32),
            jax.ShapeDtypeStruct((256, 256), F32),
            jax.ShapeDtypeStruct((64, 256), F32),
            jax.ShapeDtypeStruct((64, 64), F32),
        ],
        scratch_shapes=[
            pltpu.VMEM((32, 32, 64), F32),
            pltpu.VMEM((128, 64, 256), BF16),
            pltpu.SemaphoreType.DMA((8,)),
        ],
        compiler_params=pltpu.CompilerParams(vmem_limit_bytes=VMEM),
        name="fine",
    )(place, *operands)


def other_core(a):
    return lax.ppermute(a, "core", [(0, 1), (1, 0)])


def to_all(copies):
    mine = lax.all_to_all(copies, SAME_CORE, 0, 0, tiled=True)
    mine = mine.reshape(2, 4, 8, 8, -1)
    return mine, other_core(mine)


def body(fine_input, cotangent, lift, weight, skip, down, skip_fine):
    natural, syn_all, ana_all = _row_tables()
    col_down, col_up, col_fine = _col_tables()
    place = jnp.stack([lax.axis_index(ROWS), lax.axis_index(COLS), lax.axis_index("core")]).astype(jnp.int32)
    x = fine_input.transpose(0, 2, 1)
    u = cotangent.transpose(0, 2, 1)
    partial, ps, pst, to_modes, to_grid, to_fine, syn, ana, held = pool_call(
        place, x, natural, col_down, col_up, col_fine, syn_all, ana_all
    )
    got = lax.all_to_all(partial.reshape(128, 4, 128), ALL, 0, 0, tiled=True)
    mixed, p, s = mix_call(place, got, lift, weight)
    mine, other = to_all(mixed)
    su, sut, fine = upstream_call(held, u)
    keep, send, hl = hidden_call(
        place, mine, other, ps, pst, su, sut, lift, skip, down.T, fine, syn, ana, to_grid, to_modes
    )
    far = other_core(send)
    term = term_call(u, skip_fine)
    keep, term = lax.optimization_barrier((keep, term))
    summed = (keep + far).reshape(320, 4, 128)
    got = lax.all_to_all(summed, SAME_CORE, 0, 0, tiled=True).reshape(64, 5, 4, 128)
    pulled, block = adjoint_call(place, got, p, weight)
    mine, other = to_all(block)
    grad_spectral, narrow, lift_sum = outer_call(s, pulled, mine, lift)
    grad_input, g_lift, g_skip, g_down, g_fine = fine_call(
        place, term, hl, mine, narrow, lift_sum, other, lift, skip, syn, to_fine
    )
    return grad_input.transpose(0, 2, 1), grad_spectral, g_lift, g_skip, g_down.T, g_fine


def solution(mesh):
    split = Mesh(mesh.devices.reshape(4, 2, 2, 4, 2), ALL)
    grid = P(ROWS, COLS, None)
    modes = P(None, ALL, None, None)
    return jax.shard_map(
        body,
        mesh=split,
        in_specs=(grid, grid, P(), modes, P(), P(), P()),
        out_specs=(grid, modes, P(), P(), P(), P()),
        check_vma=False,
    )
```

```python
import math

import jax
import jax.numpy as jnp
import numpy as np
from jax import lax
from jax.experimental import pallas as pl
from jax.experimental.pallas import tpu as pltpu
from jax.sharding import Mesh, PartitionSpec as P

F32 = jnp.float32
BF16 = jnp.bfloat16
HIGH = lax.Precision.HIGHEST

ROWS = ("z", "xl", "core")
COLS = ("y", "xh")
ALL = ROWS + COLS
SAME_CORE = COLS + ("z", "xl")

PERIOD = 576
N_R, N_C = 16, 8
LR, LC = 32, 64
VMEM = 20 * 1024 * 1024


def _split(table):
    high = table.astype(BF16)
    low = (table - high.astype(np.float64)).astype(BF16)
    return high, low


def _row_tables():
    j = np.arange(32)
    f = np.where(j < 16, j, j - 32)
    n = np.arange(N_R * LR)
    angle = 2.0 * np.pi * np.mod(f[:, None] * n[None, :], PERIOD) / PERIOD
    cos = np.cos(angle).reshape(32, N_R, LR)
    sin = np.sin(angle).reshape(32, N_R, LR)
    m = np.stack([np.stack([cos, sin], -1), np.stack([-sin, cos], -1)], 0)
    m = m.transpose(2, 1, 0, 3, 4)
    full = np.einsum("rjpnq,ts->rjptnqs", m, np.eye(4))
    natural = full.transpose(0, 2, 1, 3, 4, 5, 6).reshape(N_R, 256, 256)
    split = full.reshape(N_R, 8, 2, 2, 2, 4, 256)
    split = split.transpose(0, 2, 3, 1, 4, 5, 6)
    by_core = np.stack([split[r, [r & 1, 1 - (r & 1)]] for r in range(N_R)])
    by_core = by_core.reshape(N_R, 256, 256)
    return tuple(
        np.concatenate(_split(a), -1) for a in (natural, by_core.transpose(0, 2, 1), by_core)
    )


def _col_tables():
    g = np.arange(16)
    m = np.arange(N_C * LC)
    angle = 2.0 * np.pi * np.mod(g[:, None] * m[None, :], PERIOD) / PERIOD
    both = np.stack([np.cos(angle), -np.sin(angle)], 0).reshape(2, 4, 4, N_C, LC)
    table = both.transpose(3, 1, 0, 2, 4).reshape(N_C, 32, LC)
    high, low = _split(table)
    down = np.concatenate([high, low], 1)
    up = np.concatenate([high, low, high], 1).transpose(0, 2, 1)
    wide_high, wide_low = (np.repeat(a, 4, axis=2) for a in _split(table / 16.0))
    spread = np.repeat(np.eye(LC), 4, axis=1) / 16.0
    spread = np.broadcast_to(spread.astype(BF16), (N_C, LC, 4 * LC))
    fine = np.concatenate([wide_high, wide_low, wide_high, spread], 1)
    return down, up, fine


def _dot(a, b, contract=((1,), (0,)), precision=None):
    return lax.dot_general(a, b, (contract, ((), ())), precision=precision, preferred_element_type=F32)


def _dot_nt(a, b, precision=None):
    return _dot(a, b, ((1,), (1,)), precision)


def _halves(a):
    high = a.astype(BF16)
    return high, (a - high.astype(F32)).astype(BF16)


def _turn(table, data):
    high, low = _halves(data)
    return _dot(table, jnp.concatenate([high, high], 0)) + _dot(table[:, :256], low)


def _mode_weight(place_ref):
    row = lax.broadcasted_iota(jnp.int32, (8, 256), 0)
    first = jnp.logical_and(lax.rem(row, 4) == 0, lax.rem(place_ref[1], 4) == 0)
    return jnp.where(first, 1.0, 2.0) * (1.0 / (PERIOD * PERIOD))


def _pool_matrix():
    row = lax.broadcasted_iota(jnp.int32, (512, 64), 0)
    col = lax.broadcasted_iota(jnp.int32, (512, 64), 1)
    return jnp.where(lax.rem(row, 256) // 4 == col, 1.0, 0.0).astype(BF16)


def _sum_blocks(ref, i, pool):
    rows = ref[pl.ds(i * 16, 16)].astype(F32).reshape(4, 4, 64, 256).sum(1).reshape(256, 256)
    return _dot(jnp.concatenate(_halves(rows), 1), pool)


def _pool_kernel(
    place_ref, x_any, natural_any, down_any, up_any, wide_any, syn_any, ana_any,
    p_ref, ps_ref, pst_ref, down_ref, up_ref, wide_ref, syn_ref, ana_ref, x_ref,
    rows_ref, c_ref, x_sem, sem,
):
    r, c = place_ref[0], place_ref[1]
    first = pltpu.make_async_copy(down_any.at[c], down_ref, sem.at[0])
    first.start()
    chunks = [
        pltpu.make_async_copy(x_any.at[pl.ds(32 * k, 32)], x_ref.at[pl.ds(32 * k, 32)], x_sem.at[k])
        for k in range(4)
    ]
    for chunk in chunks:
        chunk.start()
    rest = [
        pltpu.make_async_copy(source.at[at], target, sem.at[k + 1])
        for k, (source, at, target) in enumerate(
            [
                (natural_any, r, rows_ref),
                (up_any, c, up_ref),
                (wide_any, c, wide_ref),
                (syn_any, r, syn_ref),
                (ana_any, r, ana_ref),
            ]
        )
    ]
    for copy in rest:
        copy.start()
    pool = _pool_matrix()
    first.wait()
    down = down_ref[...]
    def narrow(i, xp):
        for n in range(4):
            wide = jnp.concatenate([xp[n], xp[n]], 0).astype(F32).T.astype(BF16)
            ps_ref[i * 4 + n] = wide
            modes = _dot(down, wide)
            modes = modes[:32] + modes[32:]
            at = (i * 4 + n) * 8
            for g in range(4):
                c_ref[g, at : at + 8, :] = modes[g * 8 : (g + 1) * 8]

    held = None
    for i in range(8):
        if i % 2 == 0:
            chunks[i // 2].wait()
        xp = (_sum_blocks(x_ref, i, pool) * (1.0 / 16.0)).astype(BF16)
        xp = [xp[64 * n : 64 * n + 64] for n in range(4)]
        pst_ref[:, 256 * i : 256 * (i + 1)] = jnp.concatenate(xp, 1)
        if held is not None:
            narrow(i - 1, held)
        held = xp
    narrow(7, held)
    for copy in rest:
        copy.wait()
    first_half = lax.broadcasted_iota(jnp.int32, (128, 128), 1) < 64
    for g in range(4):
        done = _turn(rows_ref[...], c_ref[g])
        done = jnp.where(first_half, done[:128], done[128:])
        p_ref[:, g] = done.reshape(32, 4, 128)


def pool_call(place, *operands):
    vm = pl.BlockSpec(memory_space=pltpu.VMEM)
    operands = [pltpu.with_memory_space_constraint(jnp.asarray(a), pltpu.HBM) for a in operands]
    return pl.pallas_call(
        _pool_kernel,
        in_specs=[pl.BlockSpec(memory_space=pltpu.SMEM)] + [pl.BlockSpec(memory_space=pltpu.HBM)] * 7,
        out_specs=[vm] * 9,
        out_shape=[
            jax.ShapeDtypeStruct((32, 4, 4, 128), F32),
            jax.ShapeDtypeStruct((32, 64, 128), BF16),
            jax.ShapeDtypeStruct((64, 2048), BF16),
            jax.ShapeDtypeStruct((64, 64), BF16),
            jax.ShapeDtypeStruct((64, 96), BF16),
            jax.ShapeDtypeStruct((160, 256), BF16),
            jax.ShapeDtypeStruct((256, 512), BF16),
            jax.ShapeDtypeStruct((256, 512), BF16),
            jax.ShapeDtypeStruct((128, 64, 256), BF16),
        ],
        scratch_shapes=[
            pltpu.VMEM((256, 512), BF16),
            pltpu.VMEM((4, 256, 128), F32),
            pltpu.SemaphoreType.DMA((4,)),
            pltpu.SemaphoreType.DMA((6,)),
        ],
        compiler_params=pltpu.CompilerParams(vmem_limit_bytes=VMEM),
        name="pool",
    )(place, *operands)


def _upstream_kernel(x_ref, u_ref, su_ref, sut_ref, fine_ref):
    pool = _pool_matrix()
    term = jnp.zeros((64, 64), F32)
    for i in range(8):
        us = _sum_blocks(u_ref, i, pool).astype(BF16)
        us = [us[64 * n : 64 * n + 64] for n in range(4)]
        sut_ref[:, 256 * i : 256 * (i + 1)] = jnp.concatenate(us, 1)
        for n in range(4):
            su_ref[i * 4 + n] = us[n].astype(F32).T.astype(BF16)
        x_all = jnp.concatenate([x_ref[i * 16 + a] for a in range(16)], 1)
        u_all = jnp.concatenate([u_ref[i * 16 + a] for a in range(16)], 1)
        term += _dot_nt(x_all, u_all)
    fine_ref[...] = term


def upstream_call(x, u):
    vm = pl.BlockSpec(memory_space=pltpu.VMEM)
    return pl.pallas_call(
        _upstream_kernel,
        in_specs=[vm] * 2,
        out_specs=[vm] * 3,
        out_shape=[
            jax.ShapeDtypeStruct((32, 64, 64), BF16),
            jax.ShapeDtypeStruct((64, 2048), BF16),
            jax.ShapeDtypeStruct((64, 64), F32),
        ],
        compiler_params=pltpu.CompilerParams(vmem_limit_bytes=VMEM),
        name="upstream",
    )(x, u)


def _mix_kernel(place_ref, got_ref, lift_ref, w_ref, mixed_ref, p_ref, s_ref):
    p = got_ref[...].sum(0)
    p = jnp.concatenate([p[:, :64], p[:, 64:]], 0)
    p_ref[...] = p
    s = _dot(jnp.concatenate(_halves(p), 0), lift_ref[...])
    s = s[:8] + s[8:]
    s_ref[...] = s
    parts = jnp.concatenate(_halves(s), 0)
    row = lax.broadcasted_iota(jnp.int32, (8, 256), 0)
    sign = jnp.where(row < 4, -1.0, 1.0)
    total = jnp.zeros((8, 256), F32)
    for t in range(4):
        a = _dot(parts, w_ref[0, t])
        b = _dot(parts, w_ref[1, t])
        a = a[:8] + a[8:]
        b = b[:8] + b[8:]
        b = jnp.concatenate([b[4:], b[:4]], 0)
        total = jnp.where(lax.rem(row, 4) == t, a + sign * b, total)
    mixed_ref[...] = jnp.broadcast_to((total * _mode_weight(place_ref))[None], (64, 8, 256))


def mix_call(place, got, lift, weight):
    vm = pl.BlockSpec(memory_space=pltpu.VMEM)
    return pl.pallas_call(
        _mix_kernel,
        in_specs=[pl.BlockSpec(memory_space=pltpu.SMEM), vm, vm, vm],
        out_specs=[vm] * 3,
        out_shape=[
            jax.ShapeDtypeStruct((64, 8, 256), F32),
            jax.ShapeDtypeStruct((8, 64), F32),
            jax.ShapeDtypeStruct((8, 256), F32),
        ],
        compiler_params=pltpu.CompilerParams(vmem_limit_bytes=VMEM),
        name="mix",
    )(place, got, lift, weight)


def _hidden_kernel(
    place_ref, mine_ref, other_ref, ps_ref, pst_ref, su_ref, sut_ref, lift_ref, skip_ref, downt_ref, fine_ref,
    syn_ref, ana_ref, up_ref, down_ref, keep_ref, send_ref, hg_ref, both_ref, t_ref, c_ref, q_ref, d_ref,
):
    for g in range(4):
        modes = jnp.concatenate([mine_ref[:, g].reshape(128, 256), other_ref[:, g].reshape(128, 256)], 0)
        turned = _turn(syn_ref[...], modes)
        t_ref[:, g * 8 : (g + 1) * 8, :] = turned.reshape(32, 8, 256)
    both = _dot(lift_ref[...], skip_ref[...])
    high, low = _halves(both)
    both_ref[...] = high
    right = jnp.concatenate([high, low], 0)
    downt = downt_ref[...]
    q_ref[...] = jnp.zeros((64, 256), F32)
    d_ref[...] = jnp.zeros((64, 256), F32)
    root = math.sqrt(2.0 / math.pi)

    def group(i, carry):
        first = _dot(ps_ref[pl.ds(i * 4, 4)].reshape(256, 128), right)
        pulled = _dot(su_ref[pl.ds(i * 4, 4)].reshape(256, 64), downt)
        field = []
        for n in range(4):
            th, tl = _halves(t_ref[i * 4 + n])
            field.append(_dot(up_ref[...], jnp.concatenate([th, th, tl], 0)))
        v = first + jnp.concatenate(field, 0)
        v2 = v * v
        half = 0.5 + 0.5 * jnp.tanh(v * (root + (root * 0.044715) * v2))
        act = (v * half).astype(BF16)
        slope = half * (1.0 + v * (2.0 * root + (6.0 * root * 0.044715) * v2) * (1.0 - half))
        hg = (pulled * slope).astype(BF16)
        lanes = pl.ds(pl.multiple_of(i * 256, 256), 256)
        q_ref[...] += _dot(pst_ref[:, lanes], hg)
        d_ref[...] += _dot(sut_ref[:, lanes], act)
        for n in range(4):
            modes = _dot(down_ref[...], hg[n * 64 : (n + 1) * 64])
            modes = modes[:32] + modes[32:]
            at = pl.multiple_of((i * 4 + n) * 8, 8)
            for g in range(4):
                c_ref[g, pl.ds(at, 8), :] = modes[g * 8 : (g + 1) * 8]
        hg_ref[lanes, :] = hg
        return carry

    lax.fori_loop(0, 8, group, 0, unroll=8)
    for g in range(4):
        done = _turn(ana_ref[...], c_ref[g])
        for ref, mine in ((keep_ref, done[:128]), (send_ref, done[128:])):
            mine = mine.reshape(2, 8, 8, 256)
            for k in range(4):
                lanes, rows = 128 * (k // 2), 4 * (k % 2)
                ref[:, g, :, k] = mine[:, :, rows : rows + 4, lanes : lanes + 128]
    core = place_ref[2]
    fine = jnp.concatenate([fine_ref[...], jnp.zeros((64, 64), F32)], 1)

    def extras(ref, low_half):
        q = jnp.where(low_half, q_ref[:, 0:128], q_ref[:, 128:256])
        d = jnp.where(low_half, d_ref[:, 0:128], d_ref[:, 128:256])
        for k, plane in enumerate((q, d, fine, jnp.zeros((64, 128), F32))):
            ref[:, :, :, 4, k, :] = plane.reshape(2, 4, 8, 128)

    extras(keep_ref, core == 0)
    extras(send_ref, core == 1)


def hidden_call(place, *operands):
    vm = pl.BlockSpec(memory_space=pltpu.VMEM)
    return pl.pallas_call(
        _hidden_kernel,
        in_specs=[pl.BlockSpec(memory_space=pltpu.SMEM)] + [vm] * 14,
        out_specs=[vm] * 4,
        out_shape=[
            jax.ShapeDtypeStruct((2, 4, 8, 5, 4, 128), F32),
            jax.ShapeDtypeStruct((2, 4, 8, 5, 4, 128), F32),
            jax.ShapeDtypeStruct((2048, 256), BF16),
            jax.ShapeDtypeStruct((64, 256), BF16),
        ],
        scratch_shapes=[
            pltpu.VMEM((32, 32, 256), F32),
            pltpu.VMEM((4, 256, 256), F32),
            pltpu.VMEM((64, 256), F32),
            pltpu.VMEM((64, 256), F32),
        ],
        compiler_params=pltpu.CompilerParams(vmem_limit_bytes=VMEM),
        name="hidden",
    )(place, *operands)


def _adjoint_kernel(place_ref, got_ref, p_ref, w_ref, pulled_ref, block_ref):
    total = got_ref[...].sum(0)
    pulled = jnp.concatenate([jnp.concatenate([total[k], total[k + 1]], 0) for k in (0, 2)], 1)
    pulled = pulled * _mode_weight(place_ref)
    sums = total[4]
    sums = jnp.concatenate(
        [sums[0:1, :64], sums[0:1, 64:], sums[1:2, :64], sums[1:2, 64:], sums[2:3, :64], jnp.zeros((3, 64), F32)], 0
    )
    pulled_ref[...] = pulled
    parts = jnp.concatenate(_halves(pulled), 0)
    row = lax.broadcasted_iota(jnp.int32, (8, 256), 0)
    sign = jnp.where(row < 4, 1.0, -1.0)
    back = jnp.zeros((8, 256), F32)
    for t in range(4):
        a = _dot_nt(parts, w_ref[0, t])
        b = _dot_nt(parts, w_ref[1, t])
        a = a[:8] + a[8:]
        b = b[:8] + b[8:]
        b = jnp.concatenate([b[4:], b[:4]], 0)
        back = jnp.where(lax.rem(row, 4) == t, a + sign * b, back)
    block = jnp.concatenate([back, p_ref[...], sums], 1)
    block_ref[...] = jnp.broadcast_to(block[None], (64, 8, 384))


def adjoint_call(place, got, p, weight):
    vm = pl.BlockSpec(memory_space=pltpu.VMEM)
    return pl.pallas_call(
        _adjoint_kernel,
        in_specs=[pl.BlockSpec(memory_space=pltpu.SMEM)] + [vm] * 3,
        out_specs=[vm] * 2,
        out_shape=[
            jax.ShapeDtypeStruct((8, 256), F32),
            jax.ShapeDtypeStruct((64, 8, 384), F32),
        ],
        compiler_params=pltpu.CompilerParams(vmem_limit_bytes=VMEM),
        name="adjoint",
    )(place, got, p, weight)


def _gathered(ref, lift):
    high, low = _halves(ref[:, :, :, :, 0:256].reshape(512, 256))
    narrow = _dot_nt(high, lift) + _dot_nt(low, lift)
    p_high, p_low = _halves(ref[:, :, :, :, 256:384].reshape(512, 128).T[:64])
    both = _dot(jnp.concatenate([p_high, p_low], 0), high)
    return narrow, both[:64] + both[64:] + _dot(p_high, low)


def _outer_kernel(s_ref, pulled_ref, mine_ref, lift_ref, grad_any, narrow_ref, sum_ref, grad_ref, sem):
    s = s_ref[...].T
    pulled = pulled_ref[...]
    copies = []
    for t in range(4):
        s0, s1 = s[:, t : t + 1], s[:, 4 + t : 5 + t]
        p0, p1 = pulled[t : t + 1], pulled[4 + t : 5 + t]
        grad_ref[0, t] = s0 * p0 + s1 * p1
        grad_ref[1, t] = s0 * p1 - s1 * p0
        for part in range(2):
            copies.append(pltpu.make_async_copy(grad_ref.at[part, t], grad_any.at[part, t], sem.at[part, t]))
            copies[-1].start()
    narrow_ref[...], sum_ref[...] = _gathered(mine_ref, lift_ref[...])
    for copy in copies:
        copy.wait()


def outer_call(s, pulled, mine, lift):
    vm = pl.BlockSpec(memory_space=pltpu.VMEM)
    return pl.pallas_call(
        _outer_kernel,
        in_specs=[vm] * 4,
        out_specs=[pl.BlockSpec(memory_space=pl.ANY), vm, vm],
        out_shape=[
            jax.ShapeDtypeStruct((2, 4, 256, 256), F32),
            jax.ShapeDtypeStruct((512, 64), F32),
            jax.ShapeDtypeStruct((64, 256), F32),
        ],
        scratch_shapes=[pltpu.VMEM((2, 4, 256, 256), F32), pltpu.SemaphoreType.DMA((2, 4))],
        compiler_params=pltpu.CompilerParams(vmem_limit_bytes=VMEM),
        cost_estimate=pl.CostEstimate(flops=2_000_000, bytes_accessed=2_200_000, transcendentals=0),
        name="outer",
    )(s, pulled, mine, lift)


def _term_kernel(u_ref, sf_ref, hg_ref, both_ref, out_ref, hl_ref):
    row = lax.broadcasted_iota(jnp.int32, (256, 256), 0)
    col = lax.broadcasted_iota(jnp.int32, (256, 256), 1)
    sf = sf_ref[...].astype(F32)
    sf = jnp.concatenate([jnp.concatenate([sf] * 4, 1)] * 4, 0)
    sf = jnp.where(row // 64 == col // 64, sf, 0.0).astype(BF16)
    for i in range(8):
        at = slice(256 * i, 256 * (i + 1))
        hl_ref[:, at] = _dot_nt(both_ref[...], hg_ref[at, :]).astype(BF16)
    for n in range(32):
        out_ref[4 * n : 4 * n + 4] = _dot(sf, u_ref[4 * n : 4 * n + 4].reshape(256, 256)).reshape(4, 64, 256)


def term_call(u, sf, hg, both):
    vm = pl.BlockSpec(memory_space=pltpu.VMEM)
    return pl.pallas_call(
        _term_kernel,
        in_specs=[vm] * 4,
        out_specs=[vm] * 2,
        out_shape=[jax.ShapeDtypeStruct((128, 64, 256), F32), jax.ShapeDtypeStruct((64, 2048), BF16)],
        compiler_params=pltpu.CompilerParams(vmem_limit_bytes=VMEM),
        cost_estimate=pl.CostEstimate(flops=400_000_000, bytes_accessed=12_000_000, transcendentals=0),
        name="term",
    )(u, sf, hg, both)


def _fine_kernel(
    place_ref, term_ref, hl_ref, mine_ref, narrow_ref, sum_ref, other_ref, lift_ref, skip_ref, syn_ref, wide_ref,
    out_any, lift_out, skip_out, down_out, fine_out, t_ref, out_ref, sem,
):
    lift = lift_ref[...]
    far_narrow, far_sum = _gathered(other_ref, lift)
    narrow = [a.reshape(2, 4, 8, 8, 64) for a in (narrow_ref[...], far_narrow)]
    for g in range(4):
        modes = jnp.concatenate([half[:, g].reshape(128, 64) for half in narrow], 0)
        t_ref[:, g * 8 : (g + 1) * 8, :] = _turn(syn_ref[...], modes).reshape(32, 8, 64)

    def chunk_copy(i):
        at = pl.ds(i * 16, 16)
        return pltpu.make_async_copy(out_ref.at[at], out_any.at[at], sem.at[i])

    def chunk(i, carry):
        hl = hl_ref[:, pl.ds(pl.multiple_of(i * 256, 256), 256)]
        th, tl = _halves(t_ref[pl.ds(i * 4, 4)].reshape(128, 64).T)
        for n in range(4):
            own = slice(32 * n, 32 * n + 32)
            left = jnp.concatenate([th[:, own], th[:, own], tl[:, own], hl[:, n * 64 : (n + 1) * 64]], 1)
            base = _dot(left, wide_ref[...])
            at = pl.ds(i * 16 + 4 * n, 4)
            out_ref[at] = (term_ref[at] + base[None]).astype(BF16)
        chunk_copy(i).start()
        return carry

    lax.fori_loop(0, 8, chunk, 0, unroll=8)
    low_core = place_ref[2] == 0
    scale = 1.0 / 512.0

    def joined(k):
        own = jnp.concatenate([mine_ref[:, :, :, j, 320:384].reshape(64, 64) for j in (k, k + 1)], 1)
        far = jnp.concatenate([other_ref[:, :, :, j, 320:384].reshape(64, 64) for j in (k, k + 1)], 1)
        return jnp.where(low_core, jnp.concatenate([own, far], 1), jnp.concatenate([far, own], 1))

    q = joined(0)
    down_out[...] = joined(2) * scale
    fine_out[...] = mine_ref[:, :, :, 4, 320:384].reshape(64, 64) * (1.0 / 2048.0)
    q_parts = jnp.concatenate(_halves(q), 0)
    tall = lift.astype(F32).T.astype(BF16)
    skip_out[...] = _dot(jnp.concatenate([tall, tall], 1), q_parts) * scale
    lift_sum = _dot_nt(q_parts, skip_ref[...])
    lift_sum = lift_sum[:64] + lift_sum[64:]
    lift_sum += sum_ref[...] + far_sum
    lift_out[...] = lift_sum * scale

    def settle(i, carry):
        chunk_copy(i).wait()
        return carry

    lax.fori_loop(0, 8, settle, 0)


def fine_call(place, *operands):
    vm = pl.BlockSpec(memory_space=pltpu.VMEM)
    return pl.pallas_call(
        _fine_kernel,
        in_specs=[pl.BlockSpec(memory_space=pltpu.SMEM)] + [vm] * 10,
        out_specs=[pl.BlockSpec(memory_space=pl.ANY)] + [vm] * 4,
        out_shape=[
            jax.ShapeDtypeStruct((128, 64, 256), BF16),
            jax.ShapeDtypeStruct((64, 256), F32),
            jax.ShapeDtypeStruct((256, 256), F32),
            jax.ShapeDtypeStruct((64, 256), F32),
            jax.ShapeDtypeStruct((64, 64), F32),
        ],
        scratch_shapes=[
            pltpu.VMEM((32, 32, 64), F32),
            pltpu.VMEM((128, 64, 256), BF16),
            pltpu.SemaphoreType.DMA((8,)),
        ],
        compiler_params=pltpu.CompilerParams(vmem_limit_bytes=VMEM),
        name="fine",
    )(place, *operands)


def other_core(a):
    return lax.ppermute(a, "core", [(0, 1), (1, 0)])


def to_all(copies):
    mine = lax.all_to_all(copies, SAME_CORE, 0, 0, tiled=True)
    mine = mine.reshape(2, 4, 8, 8, -1)
    return mine, other_core(mine)


def body(fine_input, cotangent, lift, weight, skip, down, skip_fine):
    natural, syn_all, ana_all = _row_tables()
    col_down, col_up, col_fine = _col_tables()
    place = jnp.stack([lax.axis_index(ROWS), lax.axis_index(COLS), lax.axis_index("core")]).astype(jnp.int32)
    x = fine_input.transpose(0, 2, 1)
    u = cotangent.transpose(0, 2, 1)
    partial, ps, pst, to_modes, to_grid, to_fine, syn, ana, held = pool_call(
        place, x, natural, col_down, col_up, col_fine, syn_all, ana_all
    )
    got = lax.all_to_all(partial.reshape(128, 4, 128), ALL, 0, 0, tiled=True)
    mixed, p, s = mix_call(place, got, lift, weight)
    mine, other = to_all(mixed)
    su, sut, fine = upstream_call(held, u)
    keep, send, hg, both = hidden_call(
        place, mine, other, ps, pst, su, sut, lift, skip, down.T, fine, syn, ana, to_grid, to_modes
    )
    far = other_core(send)
    term, hl = term_call(u, skip_fine, hg, both)
    keep, term = lax.optimization_barrier((keep, term))
    summed = (keep + far).reshape(320, 4, 128)
    got = lax.all_to_all(summed, SAME_CORE, 0, 0, tiled=True).reshape(64, 5, 4, 128)
    pulled, block = adjoint_call(place, got, p, weight)
    mine, other = to_all(block)
    grad_spectral, narrow, lift_sum = outer_call(s, pulled, mine, lift)
    grad_input, g_lift, g_skip, g_down, g_fine = fine_call(
        place, term, hl, mine, narrow, lift_sum, other, lift, skip, syn, to_fine
    )
    return grad_input.transpose(0, 2, 1), grad_spectral, g_lift, g_skip, g_down.T, g_fine


def solution(mesh):
    split = Mesh(mesh.devices.reshape(4, 2, 2, 4, 2), ALL)
    grid = P(ROWS, COLS, None)
    modes = P(None, ALL, None, None)
    return jax.shard_map(
        body,
        mesh=split,
        in_specs=(grid, grid, P(), modes, P(), P(), P()),
        out_specs=(grid, modes, P(), P(), P(), P()),
        check_vma=False,
    )
```

```python
import math

import jax
import jax.numpy as jnp
import numpy as np
from jax import lax
from jax.experimental import pallas as pl
from jax.experimental.pallas import tpu as pltpu
from jax.sharding import Mesh, PartitionSpec as P

F32 = jnp.float32
BF16 = jnp.bfloat16
HIGH = lax.Precision.HIGHEST

ROWS = ("z", "xl", "core")
COLS = ("y", "xh")
ALL = ROWS + COLS
SAME_CORE = COLS + ("z", "xl")

PERIOD = 576
N_R, N_C = 16, 8
LR, LC = 32, 64
VMEM = 20 * 1024 * 1024


def _split(table):
    high = table.astype(BF16)
    low = (table - high.astype(np.float64)).astype(BF16)
    return high, low


def _row_tables():
    j = np.arange(32)
    f = np.where(j < 16, j, j - 32)
    n = np.arange(N_R * LR)
    angle = 2.0 * np.pi * np.mod(f[:, None] * n[None, :], PERIOD) / PERIOD
    cos = np.cos(angle).reshape(32, N_R, LR)
    sin = np.sin(angle).reshape(32, N_R, LR)
    m = np.stack([np.stack([cos, sin], -1), np.stack([-sin, cos], -1)], 0)
    m = m.transpose(2, 1, 0, 3, 4)
    full = np.einsum("rjpnq,ts->rjptnqs", m, np.eye(4))
    natural = full.transpose(0, 2, 1, 3, 4, 5, 6).reshape(N_R, 256, 256)
    split = full.reshape(N_R, 8, 2, 2, 2, 4, 256)
    split = split.transpose(0, 2, 3, 1, 4, 5, 6)
    by_core = np.stack([split[r, [r & 1, 1 - (r & 1)]] for r in range(N_R)])
    by_core = by_core.reshape(N_R, 256, 256)
    return tuple(
        np.concatenate(_split(a), -1) for a in (natural, by_core.transpose(0, 2, 1), by_core)
    )


def _col_tables():
    g = np.arange(16)
    m = np.arange(N_C * LC)
    angle = 2.0 * np.pi * np.mod(g[:, None] * m[None, :], PERIOD) / PERIOD
    both = np.stack([np.cos(angle), -np.sin(angle)], 0).reshape(2, 4, 4, N_C, LC)
    table = both.transpose(3, 1, 0, 2, 4).reshape(N_C, 32, LC)
    high, low = _split(table)
    down = np.concatenate([high, low], 1)
    up = np.concatenate([high, low, high], 1).transpose(0, 2, 1)
    wide_high, wide_low = (np.repeat(a, 4, axis=2) for a in _split(table / 16.0))
    spread = np.repeat(np.eye(LC), 4, axis=1) / 16.0
    spread = np.broadcast_to(spread.astype(BF16), (N_C, LC, 4 * LC))
    fine = np.concatenate([wide_high, wide_low, wide_high, spread], 1)
    return down, up, fine


def _dot(a, b, contract=((1,), (0,)), precision=None):
    return lax.dot_general(a, b, (contract, ((), ())), precision=precision, preferred_element_type=F32)


def _dot_nt(a, b, precision=None):
    return _dot(a, b, ((1,), (1,)), precision)


def _halves(a):
    high = a.astype(BF16)
    return high, (a - high.astype(F32)).astype(BF16)


def _turn(table, data):
    high, low = _halves(data)
    return _dot(table, jnp.concatenate([high, high], 0)) + _dot(table[:, :256], low)


def _mode_weight(place_ref):
    row = lax.broadcasted_iota(jnp.int32, (8, 256), 0)
    first = jnp.logical_and(lax.rem(row, 4) == 0, lax.rem(place_ref[1], 4) == 0)
    return jnp.where(first, 1.0, 2.0) * (1.0 / (PERIOD * PERIOD))


def _pool_matrix():
    row = lax.broadcasted_iota(jnp.int32, (512, 64), 0)
    col = lax.broadcasted_iota(jnp.int32, (512, 64), 1)
    return jnp.where(lax.rem(row, 256) // 4 == col, 1.0, 0.0).astype(BF16)


def _sum_blocks(ref, i, pool):
    rows = ref[pl.ds(i * 16, 16)].astype(F32).reshape(4, 4, 64, 256).sum(1).reshape(256, 256)
    return _dot(jnp.concatenate(_halves(rows), 1), pool)


def _pool_kernel(
    place_ref, x_any, natural_any, down_any, up_any, wide_any, syn_any, ana_any,
    p_ref, ps_ref, pst_ref, down_ref, up_ref, wide_ref, syn_ref, ana_ref, x_ref,
    rows_ref, c_ref, x_sem, sem,
):
    r, c = place_ref[0], place_ref[1]
    first = pltpu.make_async_copy(down_any.at[c], down_ref, sem.at[0])
    first.start()
    chunks = [
        pltpu.make_async_copy(x_any.at[pl.ds(32 * k, 32)], x_ref.at[pl.ds(32 * k, 32)], x_sem.at[k])
        for k in range(4)
    ]
    for chunk in chunks:
        chunk.start()
    rest = [
        pltpu.make_async_copy(source.at[at], target, sem.at[k + 1])
        for k, (source, at, target) in enumerate(
            [
                (natural_any, r, rows_ref),
                (up_any, c, up_ref),
                (wide_any, c, wide_ref),
                (syn_any, r, syn_ref),
                (ana_any, r, ana_ref),
            ]
        )
    ]
    for copy in rest:
        copy.start()
    pool = _pool_matrix()
    first.wait()
    down = down_ref[...]
    def narrow(i, xp):
        for n in range(4):
            wide = jnp.concatenate([xp[n], xp[n]], 0).astype(F32).T.astype(BF16)
            ps_ref[i * 4 + n] = wide
            modes = _dot(down, wide)
            modes = modes[:32] + modes[32:]
            at = (i * 4 + n) * 8
            for g in range(4):
                c_ref[g, at : at + 8, :] = modes[g * 8 : (g + 1) * 8]

    held = None
    for i in range(8):
        if i % 2 == 0:
            chunks[i // 2].wait()
        xp = (_sum_blocks(x_ref, i, pool) * (1.0 / 16.0)).astype(BF16)
        xp = [xp[64 * n : 64 * n + 64] for n in range(4)]
        pst_ref[:, 256 * i : 256 * (i + 1)] = jnp.concatenate(xp, 1)
        if held is not None:
            narrow(i - 1, held)
        held = xp
    narrow(7, held)
    for copy in rest:
        copy.wait()
    first_half = lax.broadcasted_iota(jnp.int32, (128, 128), 1) < 64
    for g in range(4):
        done = _turn(rows_ref[...], c_ref[g])
        done = jnp.where(first_half, done[:128], done[128:])
        p_ref[:, g] = done.reshape(32, 4, 128)


def pool_call(place, *operands):
    vm = pl.BlockSpec(memory_space=pltpu.VMEM)
    operands = [pltpu.with_memory_space_constraint(jnp.asarray(a), pltpu.HBM) for a in operands]
    return pl.pallas_call(
        _pool_kernel,
        in_specs=[pl.BlockSpec(memory_space=pltpu.SMEM)] + [pl.BlockSpec(memory_space=pltpu.HBM)] * 7,
        out_specs=[vm] * 9,
        out_shape=[
            jax.ShapeDtypeStruct((32, 4, 4, 128), F32),
            jax.ShapeDtypeStruct((32, 64, 128), BF16),
            jax.ShapeDtypeStruct((64, 2048), BF16),
            jax.ShapeDtypeStruct((64, 64), BF16),
            jax.ShapeDtypeStruct((64, 96), BF16),
            jax.ShapeDtypeStruct((160, 256), BF16),
            jax.ShapeDtypeStruct((256, 512), BF16),
            jax.ShapeDtypeStruct((256, 512), BF16),
            jax.ShapeDtypeStruct((128, 64, 256), BF16),
        ],
        scratch_shapes=[
            pltpu.VMEM((256, 512), BF16),
            pltpu.VMEM((4, 256, 128), F32),
            pltpu.SemaphoreType.DMA((4,)),
            pltpu.SemaphoreType.DMA((6,)),
        ],
        compiler_params=pltpu.CompilerParams(vmem_limit_bytes=VMEM),
        name="pool",
    )(place, *operands)


def _upstream_kernel(x_ref, u_ref, su_ref, sut_ref, fine_ref):
    pool = _pool_matrix()
    term = jnp.zeros((64, 64), F32)
    for i in range(8):
        us = _sum_blocks(u_ref, i, pool).astype(BF16)
        us = [us[64 * n : 64 * n + 64] for n in range(4)]
        sut_ref[:, 256 * i : 256 * (i + 1)] = jnp.concatenate(us, 1)
        for n in range(4):
            su_ref[i * 4 + n] = us[n].astype(F32).T.astype(BF16)
        x_all = jnp.concatenate([x_ref[i * 16 + a] for a in range(16)], 1)
        u_all = jnp.concatenate([u_ref[i * 16 + a] for a in range(16)], 1)
        term += _dot_nt(x_all, u_all)
    fine_ref[...] = term


def upstream_call(x, u):
    vm = pl.BlockSpec(memory_space=pltpu.VMEM)
    return pl.pallas_call(
        _upstream_kernel,
        in_specs=[vm] * 2,
        out_specs=[vm] * 3,
        out_shape=[
            jax.ShapeDtypeStruct((32, 64, 64), BF16),
            jax.ShapeDtypeStruct((64, 2048), BF16),
            jax.ShapeDtypeStruct((64, 64), F32),
        ],
        compiler_params=pltpu.CompilerParams(vmem_limit_bytes=VMEM),
        name="upstream",
    )(x, u)


def _mix_kernel(place_ref, got_ref, lift_ref, w_ref, mixed_ref, p_ref, s_ref):
    p = got_ref[...].sum(0)
    p = jnp.concatenate([p[:, :64], p[:, 64:]], 0)
    p_ref[...] = p
    s = _dot(jnp.concatenate(_halves(p), 0), lift_ref[...])
    s = s[:8] + s[8:]
    s_ref[...] = s
    parts = jnp.concatenate(_halves(s), 0)
    row = lax.broadcasted_iota(jnp.int32, (8, 256), 0)
    sign = jnp.where(row < 4, -1.0, 1.0)
    total = jnp.zeros((8, 256), F32)
    for t in range(4):
        a = _dot(parts, w_ref[0, t])
        b = _dot(parts, w_ref[1, t])
        a = a[:8] + a[8:]
        b = b[:8] + b[8:]
        b = jnp.concatenate([b[4:], b[:4]], 0)
        total = jnp.where(lax.rem(row, 4) == t, a + sign * b, total)
    mixed_ref[...] = jnp.broadcast_to((total * _mode_weight(place_ref))[None], (64, 8, 256))


def mix_call(place, got, lift, weight):
    vm = pl.BlockSpec(memory_space=pltpu.VMEM)
    return pl.pallas_call(
        _mix_kernel,
        in_specs=[pl.BlockSpec(memory_space=pltpu.SMEM), vm, vm, vm],
        out_specs=[vm] * 3,
        out_shape=[
            jax.ShapeDtypeStruct((64, 8, 256), F32),
            jax.ShapeDtypeStruct((8, 64), F32),
            jax.ShapeDtypeStruct((8, 256), F32),
        ],
        compiler_params=pltpu.CompilerParams(vmem_limit_bytes=VMEM),
        name="mix",
    )(place, got, lift, weight)


def _hidden_kernel(
    place_ref, mine_ref, other_ref, ps_ref, pst_ref, su_ref, sut_ref, lift_ref, skip_ref, downt_ref, fine_ref,
    syn_ref, ana_ref, up_ref, down_ref, keep_ref, send_ref, hg_ref, both_ref, t_ref, c_ref, q_ref, d_ref,
):
    for g in range(4):
        modes = jnp.concatenate([mine_ref[:, g].reshape(128, 256), other_ref[:, g].reshape(128, 256)], 0)
        turned = _turn(syn_ref[...], modes)
        t_ref[:, g * 8 : (g + 1) * 8, :] = turned.reshape(32, 8, 256)
    both = _dot(lift_ref[...], skip_ref[...])
    high, low = _halves(both)
    both_ref[...] = high
    right = jnp.concatenate([high, low], 0)
    downt = downt_ref[...]
    q_ref[...] = jnp.zeros((64, 256), F32)
    d_ref[...] = jnp.zeros((64, 256), F32)
    root = math.sqrt(2.0 / math.pi)

    def group(i, carry):
        first = _dot(ps_ref[pl.ds(i * 4, 4)].reshape(256, 128), right)
        pulled = _dot(su_ref[pl.ds(i * 4, 4)].reshape(256, 64), downt)
        field = []
        for n in range(4):
            th, tl = _halves(t_ref[i * 4 + n])
            field.append(_dot(up_ref[...], jnp.concatenate([th, th, tl], 0)))
        v = first + jnp.concatenate(field, 0)
        v2 = v * v
        half = 0.5 + 0.5 * jnp.tanh(v * (root + (root * 0.044715) * v2))
        act = (v * half).astype(BF16)
        slope = half * (1.0 + v * (2.0 * root + (6.0 * root * 0.044715) * v2) * (1.0 - half))
        hg = (pulled * slope).astype(BF16)
        lanes = pl.ds(pl.multiple_of(i * 256, 256), 256)
        q_ref[...] += _dot(pst_ref[:, lanes], hg)
        d_ref[...] += _dot(sut_ref[:, lanes], act)
        for n in range(4):
            modes = _dot(down_ref[...], hg[n * 64 : (n + 1) * 64])
            modes = modes[:32] + modes[32:]
            at = pl.multiple_of((i * 4 + n) * 8, 8)
            for g in range(4):
                c_ref[g, pl.ds(at, 8), :] = modes[g * 8 : (g + 1) * 8]
        hg_ref[lanes, :] = hg
        return carry

    lax.fori_loop(0, 8, group, 0, unroll=8)
    for g in range(4):
        done = _turn(ana_ref[...], c_ref[g])
        for ref, mine in ((keep_ref, done[:128]), (send_ref, done[128:])):
            mine = mine.reshape(2, 8, 8, 256)
            for k in range(4):
                lanes, rows = 128 * (k // 2), 4 * (k % 2)
                ref[:, g, :, k] = mine[:, :, rows : rows + 4, lanes : lanes + 128]
    core = place_ref[2]
    fine = jnp.concatenate([fine_ref[...], jnp.zeros((64, 64), F32)], 1)

    def extras(ref, low_half):
        q = jnp.where(low_half, q_ref[:, 0:128], q_ref[:, 128:256])
        d = jnp.where(low_half, d_ref[:, 0:128], d_ref[:, 128:256])
        for k, plane in enumerate((q, d, fine, jnp.zeros((64, 128), F32))):
            ref[:, :, :, 4, k, :] = plane.reshape(2, 4, 8, 128)

    extras(keep_ref, core == 0)
    extras(send_ref, core == 1)


def hidden_call(place, *operands):
    vm = pl.BlockSpec(memory_space=pltpu.VMEM)
    return pl.pallas_call(
        _hidden_kernel,
        in_specs=[pl.BlockSpec(memory_space=pltpu.SMEM)] + [vm] * 14,
        out_specs=[vm] * 4,
        out_shape=[
            jax.ShapeDtypeStruct((2, 4, 8, 5, 4, 128), F32),
            jax.ShapeDtypeStruct((2, 4, 8, 5, 4, 128), F32),
            jax.ShapeDtypeStruct((2048, 256), BF16),
            jax.ShapeDtypeStruct((64, 256), BF16),
        ],
        scratch_shapes=[
            pltpu.VMEM((32, 32, 256), F32),
            pltpu.VMEM((4, 256, 256), F32),
            pltpu.VMEM((64, 256), F32),
            pltpu.VMEM((64, 256), F32),
        ],
        compiler_params=pltpu.CompilerParams(vmem_limit_bytes=VMEM),
        name="hidden",
    )(place, *operands)


def _adjoint_kernel(place_ref, got_ref, p_ref, w_ref, pulled_ref, block_ref):
    total = got_ref[...].sum(0)
    pulled = jnp.concatenate([jnp.concatenate([total[k], total[k + 1]], 0) for k in (0, 2)], 1)
    pulled = pulled * _mode_weight(place_ref)
    sums = total[4]
    sums = jnp.concatenate(
        [sums[0:1, :64], sums[0:1, 64:], sums[1:2, :64], sums[1:2, 64:], sums[2:3, :64], jnp.zeros((3, 64), F32)], 0
    )
    pulled_ref[...] = pulled
    parts = jnp.concatenate(_halves(pulled), 0)
    row = lax.broadcasted_iota(jnp.int32, (8, 256), 0)
    sign = jnp.where(row < 4, 1.0, -1.0)
    back = jnp.zeros((8, 256), F32)
    for t in range(4):
        a = _dot_nt(parts, w_ref[0, t])
        b = _dot_nt(parts, w_ref[1, t])
        a = a[:8] + a[8:]
        b = b[:8] + b[8:]
        b = jnp.concatenate([b[4:], b[:4]], 0)
        back = jnp.where(lax.rem(row, 4) == t, a + sign * b, back)
    block = jnp.concatenate([back, p_ref[...], sums], 1)
    block_ref[...] = jnp.broadcast_to(block[None], (64, 8, 384))


def adjoint_call(place, got, p, weight):
    vm = pl.BlockSpec(memory_space=pltpu.VMEM)
    return pl.pallas_call(
        _adjoint_kernel,
        in_specs=[pl.BlockSpec(memory_space=pltpu.SMEM)] + [vm] * 3,
        out_specs=[vm] * 2,
        out_shape=[
            jax.ShapeDtypeStruct((8, 256), F32),
            jax.ShapeDtypeStruct((64, 8, 384), F32),
        ],
        compiler_params=pltpu.CompilerParams(vmem_limit_bytes=VMEM),
        name="adjoint",
    )(place, got, p, weight)


def _gathered(ref, lift):
    high, low = _halves(ref[:, :, :, :, 0:256].reshape(512, 256))
    narrow = _dot_nt(high, lift) + _dot_nt(low, lift)
    p_high, p_low = _halves(ref[:, :, :, :, 256:384].reshape(512, 128).T[:64])
    both = _dot(jnp.concatenate([p_high, p_low], 0), high)
    return narrow, both[:64] + both[64:] + _dot(p_high, low)


def _turn_class(table_ref, apart, narrow, g):
    table_high = table_ref[:, 128 * apart : 128 * apart + 128]
    table_low = table_ref[:, 256 + 128 * apart : 384 + 128 * apart]
    high, low = _halves(narrow.reshape(2, 4, 8, 8, 64)[:, g].reshape(128, 64))
    turned = _dot(jnp.concatenate([table_high, table_low], 1), jnp.concatenate([high, high], 0))
    return (turned + _dot(table_high, low)).reshape(32, 8, 64)


def _outer_kernel(s_ref, pulled_ref, mine_ref, lift_ref, syn_ref, grad_any, near_ref, sum_ref, grad_ref, sem):
    s = s_ref[...].T
    pulled = pulled_ref[...]
    copies = []
    for t in range(4):
        s0, s1 = s[:, t : t + 1], s[:, 4 + t : 5 + t]
        p0, p1 = pulled[t : t + 1], pulled[4 + t : 5 + t]
        grad_ref[0, t] = s0 * p0 + s1 * p1
        grad_ref[1, t] = s0 * p1 - s1 * p0
        for part in range(2):
            copies.append(pltpu.make_async_copy(grad_ref.at[part, t], grad_any.at[part, t], sem.at[part, t]))
            copies[-1].start()
    narrow, sum_ref[...] = _gathered(mine_ref, lift_ref[...])
    for g in range(4):
        near_ref[:, g * 8 : (g + 1) * 8, :] = _turn_class(syn_ref, 0, narrow, g)
    for copy in copies:
        copy.wait()


def outer_call(s, pulled, mine, lift, syn):
    vm = pl.BlockSpec(memory_space=pltpu.VMEM)
    return pl.pallas_call(
        _outer_kernel,
        in_specs=[vm] * 5,
        out_specs=[pl.BlockSpec(memory_space=pl.ANY), vm, vm],
        out_shape=[
            jax.ShapeDtypeStruct((2, 4, 256, 256), F32),
            jax.ShapeDtypeStruct((32, 32, 64), F32),
            jax.ShapeDtypeStruct((64, 256), F32),
        ],
        scratch_shapes=[pltpu.VMEM((2, 4, 256, 256), F32), pltpu.SemaphoreType.DMA((2, 4))],
        compiler_params=pltpu.CompilerParams(vmem_limit_bytes=VMEM),
        cost_estimate=pl.CostEstimate(flops=2_000_000, bytes_accessed=2_200_000, transcendentals=0),
        name="outer",
    )(s, pulled, mine, lift, syn)


def _term_kernel(u_ref, sf_ref, hg_ref, both_ref, out_ref, hl_ref):
    row = lax.broadcasted_iota(jnp.int32, (256, 256), 0)
    col = lax.broadcasted_iota(jnp.int32, (256, 256), 1)
    sf = sf_ref[...].astype(F32)
    sf = jnp.concatenate([jnp.concatenate([sf] * 4, 1)] * 4, 0)
    sf = jnp.where(row // 64 == col // 64, sf, 0.0).astype(BF16)
    for i in range(8):
        at = slice(256 * i, 256 * (i + 1))
        hl_ref[:, at] = _dot_nt(both_ref[...], hg_ref[at, :]).astype(BF16)
    for n in range(32):
        out_ref[4 * n : 4 * n + 4] = _dot(sf, u_ref[4 * n : 4 * n + 4].reshape(256, 256)).reshape(4, 64, 256)


def term_call(u, sf, hg, both):
    vm = pl.BlockSpec(memory_space=pltpu.VMEM)
    return pl.pallas_call(
        _term_kernel,
        in_specs=[vm] * 4,
        out_specs=[vm] * 2,
        out_shape=[jax.ShapeDtypeStruct((128, 64, 256), F32), jax.ShapeDtypeStruct((64, 2048), BF16)],
        compiler_params=pltpu.CompilerParams(vmem_limit_bytes=VMEM),
        cost_estimate=pl.CostEstimate(flops=400_000_000, bytes_accessed=12_000_000, transcendentals=0),
        name="term",
    )(u, sf, hg, both)


def _fine_kernel(
    place_ref, term_ref, hl_ref, mine_ref, near_ref, sum_ref, other_ref, lift_ref, skip_ref, syn_ref, wide_ref,
    out_any, lift_out, skip_out, down_out, fine_out, t_ref, out_ref, sem,
):
    lift = lift_ref[...]
    far_narrow, far_sum = _gathered(other_ref, lift)
    for g in range(4):
        own = slice(g * 8, (g + 1) * 8)
        t_ref[:, own, :] = near_ref[:, own, :] + _turn_class(syn_ref, 1, far_narrow, g)

    def chunk_copy(i):
        at = pl.ds(i * 16, 16)
        return pltpu.make_async_copy(out_ref.at[at], out_any.at[at], sem.at[i])

    def chunk(i, carry):
        hl = hl_ref[:, pl.ds(pl.multiple_of(i * 256, 256), 256)]
        th, tl = _halves(t_ref[pl.ds(i * 4, 4)].reshape(128, 64).T)
        for n in range(4):
            own = slice(32 * n, 32 * n + 32)
            left = jnp.concatenate([th[:, own], th[:, own], tl[:, own], hl[:, n * 64 : (n + 1) * 64]], 1)
            base = _dot(left, wide_ref[...])
            at = pl.ds(i * 16 + 4 * n, 4)
            out_ref[at] = (term_ref[at] + base[None]).astype(BF16)
        chunk_copy(i).start()
        return carry

    lax.fori_loop(0, 8, chunk, 0, unroll=8)
    low_core = place_ref[2] == 0
    scale = 1.0 / 512.0

    def joined(k):
        own = jnp.concatenate([mine_ref[:, :, :, j, 320:384].reshape(64, 64) for j in (k, k + 1)], 1)
        far = jnp.concatenate([other_ref[:, :, :, j, 320:384].reshape(64, 64) for j in (k, k + 1)], 1)
        return jnp.where(low_core, jnp.concatenate([own, far], 1), jnp.concatenate([far, own], 1))

    q = joined(0)
    down_out[...] = joined(2) * scale
    fine_out[...] = mine_ref[:, :, :, 4, 320:384].reshape(64, 64) * (1.0 / 2048.0)
    q_parts = jnp.concatenate(_halves(q), 0)
    tall = lift.astype(F32).T.astype(BF16)
    skip_out[...] = _dot(jnp.concatenate([tall, tall], 1), q_parts) * scale
    lift_sum = _dot_nt(q_parts, skip_ref[...])
    lift_sum = lift_sum[:64] + lift_sum[64:]
    lift_sum += sum_ref[...] + far_sum
    lift_out[...] = lift_sum * scale

    def settle(i, carry):
        chunk_copy(i).wait()
        return carry

    lax.fori_loop(0, 8, settle, 0)


def fine_call(place, *operands):
    vm = pl.BlockSpec(memory_space=pltpu.VMEM)
    return pl.pallas_call(
        _fine_kernel,
        in_specs=[pl.BlockSpec(memory_space=pltpu.SMEM)] + [vm] * 10,
        out_specs=[pl.BlockSpec(memory_space=pl.ANY)] + [vm] * 4,
        out_shape=[
            jax.ShapeDtypeStruct((128, 64, 256), BF16),
            jax.ShapeDtypeStruct((64, 256), F32),
            jax.ShapeDtypeStruct((256, 256), F32),
            jax.ShapeDtypeStruct((64, 256), F32),
            jax.ShapeDtypeStruct((64, 64), F32),
        ],
        scratch_shapes=[
            pltpu.VMEM((32, 32, 64), F32),
            pltpu.VMEM((128, 64, 256), BF16),
            pltpu.SemaphoreType.DMA((8,)),
        ],
        compiler_params=pltpu.CompilerParams(vmem_limit_bytes=VMEM),
        name="fine",
    )(place, *operands)


def other_core(a):
    return lax.ppermute(a, "core", [(0, 1), (1, 0)])


def to_all(copies):
    mine = lax.all_to_all(copies, SAME_CORE, 0, 0, tiled=True)
    mine = mine.reshape(2, 4, 8, 8, -1)
    return mine, other_core(mine)


def body(fine_input, cotangent, lift, weight, skip, down, skip_fine):
    natural, syn_all, ana_all = _row_tables()
    col_down, col_up, col_fine = _col_tables()
    place = jnp.stack([lax.axis_index(ROWS), lax.axis_index(COLS), lax.axis_index("core")]).astype(jnp.int32)
    x = fine_input.transpose(0, 2, 1)
    u = cotangent.transpose(0, 2, 1)
    partial, ps, pst, to_modes, to_grid, to_fine, syn, ana, held = pool_call(
        place, x, natural, col_down, col_up, col_fine, syn_all, ana_all
    )
    got = lax.all_to_all(partial.reshape(128, 4, 128), ALL, 0, 0, tiled=True)
    mixed, p, s = mix_call(place, got, lift, weight)
    mine, other = to_all(mixed)
    su, sut, fine = upstream_call(held, u)
    keep, send, hg, both = hidden_call(
        place, mine, other, ps, pst, su, sut, lift, skip, down.T, fine, syn, ana, to_grid, to_modes
    )
    far = other_core(send)
    term, hl = term_call(u, skip_fine, hg, both)
    keep, term = lax.optimization_barrier((keep, term))
    summed = (keep + far).reshape(320, 4, 128)
    got = lax.all_to_all(summed, SAME_CORE, 0, 0, tiled=True).reshape(64, 5, 4, 128)
    pulled, block = adjoint_call(place, got, p, weight)
    mine, other = to_all(block)
    grad_spectral, near, lift_sum = outer_call(s, pulled, mine, lift, syn)
    grad_input, g_lift, g_skip, g_down, g_fine = fine_call(
        place, term, hl, mine, near, lift_sum, other, lift, skip, syn, to_fine
    )
    return grad_input.transpose(0, 2, 1), grad_spectral, g_lift, g_skip, g_down.T, g_fine


def solution(mesh):
    split = Mesh(mesh.devices.reshape(4, 2, 2, 4, 2), ALL)
    grid = P(ROWS, COLS, None)
    modes = P(None, ALL, None, None)
    return jax.shard_map(
        body,
        mesh=split,
        in_specs=(grid, grid, P(), modes, P(), P(), P()),
        out_specs=(grid, modes, P(), P(), P(), P()),
        check_vma=False,
    )
```
